512 devices in a mesh: seq: 64 (over z, y_hi, core), head: 8 (over y_lo, x).
Axes of the slice: x: 4, y: 8 (y_hi: 4, y_lo: 2; y = y_hi * 2 + y_lo), z: 8, core: 2. Of those that a mesh axis runs over, the one named last changes fastest.
Arguments:
- noisy_q: bfloat16 [16640, 3072], P('seq', 'head'), may hold values from -38 to 38
- noisy_k: bfloat16 [16640, 1024], P('seq', 'head'), may hold values from -38 to 38
- noisy_value: bfloat16 [16640, 1024], P('seq', 'head'), may hold values from -6 to 6
- clean_k: bfloat16 [16640, 1024], P('seq', 'head'), may hold values from -38 to 38
- clean_value: bfloat16 [16640, 1024], P('seq', 'head'), may hold values from -6 to 6
- q_gain: float32 [3072], P('head'), may hold values from 0.1 to 1.9
- key_norm_gain: float32 [1024], P('head'), may hold values from 0.1 to 1.9
- out_grad: bfloat16 [16640, 3072], P('seq', 'head'), may hold values from -18 to 18
- window: int32 [32, 2], replicated, may hold values from -1 to 30, as said below
Outputs:
- attn_out: bfloat16 [16640, 3072], P('seq', 'head')
- grad_q: bfloat16 [16640, 3072], P('seq', 'head')
- grad_k: bfloat16 [16640, 1024], P('seq', 'head')
- grad_v: bfloat16 [16640, 1024], P('seq', 'head')
- grad_clean_k: bfloat16 [16640, 1024], P('seq', 'head')
- grad_clean_v: bfloat16 [16640, 1024], P('seq', 'head')
The draws below stay inside these ranges and needn't reach their ends.
Inputs may be any that keep to these rules, and one draw needn't show every extreme that they name: `window`: row c lists, in an order drawn from the seed, the clean stretch c - 1 and one clean stretch from c - 3 to c - 2 that is 0 or later; an entry is -1 where no such stretch exists.
All inputs are finite; a program needn't handle non-finite values.
Results may differ from the reference program's by a relative error of at most 0.04.
Values may be sent and summed in bfloat16 or wider, within the bound.
No kernel may reach another device: no remote copies, remote signals or barrier semaphores. Data moves between devices by JAX's collectives and lax.ppermute only.
A program may use at most 64 MiB of HBM per device.

```python
import math
import jax
import jax.numpy as jnp
from jax import lax

HEAD_SIZE = 128
KEY_VALUE_HEADS = 8
GROUP = 3
STRETCH = 520
WINDOW = 3
SLOTS = 2
HQ = 24
NCH = 32
TOKEN_COUNT = 16640


def feature_scales(count, ratio):
    column = jnp.arange(count, dtype=jnp.int32)
    spots = (column * 37 % HEAD_SIZE).astype(jnp.float32) / max(HEAD_SIZE - 1, 1)
    return jnp.exp(math.log(ratio) * (spots - 0.5))


def block_scaled(key, rows_total, cols_total):
    first_key, second_key = jax.random.split(key)
    basis = jax.random.truncated_normal(first_key, -4.0, 4.0, (rows_total, cols_total), jnp.float32)
    ratio = 10.0
    row_scale = jnp.exp(jax.random.uniform(second_key, (rows_total, 1), jnp.float32, math.log(0.3), math.log(3.0)))
    return basis * row_scale * feature_scales(cols_total, ratio)[None, :]


def draw_noisy_q(key, part):
    block_tile = block_scaled(jax.random.fold_in(key, 1), TOKEN_COUNT, HQ * HEAD_SIZE)
    return block_tile.astype(jnp.bfloat16)


def draw_noisy_k(key, part):
    block_tile = block_scaled(jax.random.fold_in(key, 2), TOKEN_COUNT, KEY_VALUE_HEADS * HEAD_SIZE)
    return block_tile.astype(jnp.bfloat16)


def draw_clean_k(key, part):
    return block_scaled(jax.random.fold_in(key, 3), TOKEN_COUNT, KEY_VALUE_HEADS * HEAD_SIZE).astype(jnp.bfloat16)


def draw_window(key, part):
    stretch_ids = jnp.arange(NCH, dtype=jnp.int32)
    first_key, second_key = jax.random.split(jax.random.fold_in(key, 9))
    previous = jnp.where(stretch_ids >= 1, stretch_ids - 1, -1)
    reach_back = jnp.clip(stretch_ids - 1, 1, WINDOW - 1)
    back_by = jax.random.randint(first_key, (NCH,), 0, reach_back)
    other = stretch_ids - 2 - back_by
    other = jnp.where(other >= 0, other, -1)
    flipped = jax.random.randint(second_key, (NCH,), 0, 2)
    first_col = jnp.where(flipped == 1, other, previous)
    second_col = jnp.where(flipped == 1, previous, other)
    return jnp.stack([first_col, second_col], axis=1).astype(jnp.int32)


def level_of(own_key, extent, shards, least, largest):
    loudness = 1.0
    for axis_at, shards_of in shards:
        draws = jax.random.uniform(jax.random.fold_in(jax.random.fold_in(own_key, 6), axis_at), (shards_of,), jnp.float32, least / len(shards), largest / len(shards))
        loudness = loudness * jnp.repeat(jnp.exp(draws), extent[axis_at] // shards_of).reshape((-1,) + (1,) * (len(extent) - 1 - axis_at))
    return loudness


def centred(stream_key, dims, deviation, limit, shards=(), kind=jnp.bfloat16):
    entries = jax.random.normal(stream_key, dims, jnp.float32) * deviation
    if len(shards) > 0:
        entries = level_of(stream_key, dims, shards, -0.22, 0.18) * entries
    return jnp.clip(entries, min=-limit, max=limit).astype(kind)


def setup_inputs(seed: int = 0) -> dict:
    splits = jax.random.split(jax.random.key(seed), 10)
    return {
        "noisy_q": draw_noisy_q(jax.random.fold_in(splits[9], 71), 0),
        "noisy_k": draw_noisy_k(jax.random.fold_in(splits[9], 71), 0),
        "noisy_value": centred(splits[2], (TOKEN_COUNT, KEY_VALUE_HEADS * HEAD_SIZE), 1.0, 6.0, ((0, 64), (1, 8))),
        "clean_k": draw_clean_k(jax.random.fold_in(splits[9], 71), 0),
        "clean_value": centred(splits[4], (TOKEN_COUNT, KEY_VALUE_HEADS * HEAD_SIZE), 1.0, 6.0, ((0, 64), (1, 8))),
        "q_gain": jnp.clip(1.0 + 0.18 * jax.random.normal(splits[5], (HQ * HEAD_SIZE,), jnp.float32), 0.1, 1.9),
        "key_norm_gain": jnp.clip(1.0 + 0.18 * jax.random.normal(splits[6], (KEY_VALUE_HEADS * HEAD_SIZE,), jnp.float32), 0.1, 1.9),
        "out_grad": centred(splits[7], (TOKEN_COUNT, HQ * HEAD_SIZE), 3.0, 18.0, ((0, 64), (1, 8))),
        "window": draw_window(jax.random.fold_in(splits[9], 71), 0),
    }


EPSILON = 1e-06
NEG_FILL = -1e+30

def normalize(raw_rows, gain_vec):
    full_rows = raw_rows.astype(jnp.float32)
    inv_rms = lax.rsqrt(lax.optimization_barrier(jnp.mean(full_rows * full_rows, axis=1, keepdims=True)) + EPSILON)
    return ((full_rows * inv_rms * gain_vec[None, :]).astype(jnp.bfloat16), inv_rms)

def norm_grad(raw_rows, gain_vec, inv_rms, grad_rows):
    full_rows = raw_rows.astype(jnp.float32)
    scaled = grad_rows * gain_vec[None, :]
    inner_sum = lax.optimization_barrier(jnp.mean(scaled * full_rows, axis=1, keepdims=True))
    return (inv_rms * scaled - full_rows * inv_rms * inv_rms * inv_rms * inner_sum).astype(jnp.bfloat16)

def stretch_attention(q_rows, grad_rows, every_key, key_mask):
    score_scale = HEAD_SIZE ** (-0.5)
    out_parts, dq_parts, dk_parts, dv_parts = ([], [], [], [])
    for key_value_head in range(KEY_VALUE_HEADS):
        key_cols = every_key[:, key_value_head * HEAD_SIZE:(key_value_head + 1) * HEAD_SIZE]
        value_columns = every_key[:, (KEY_VALUE_HEADS + key_value_head) * HEAD_SIZE:(KEY_VALUE_HEADS + key_value_head + 1) * HEAD_SIZE]
        first_col = key_value_head * GROUP * HEAD_SIZE
        last_col = (key_value_head + 1) * GROUP * HEAD_SIZE
        query_rows = q_rows[:, first_col:last_col].reshape(-1, HEAD_SIZE)
        out_grads = grad_rows[:, first_col:last_col].reshape(-1, HEAD_SIZE)
        scores = jnp.dot(query_rows, key_cols.T, preferred_element_type=jnp.float32) * score_scale
        scores = jnp.where(key_mask[None, :], scores, NEG_FILL)
        row_max = lax.optimization_barrier(jnp.max(scores, axis=1, keepdims=True))
        weights = jnp.exp(scores - row_max)
        probs = weights / lax.optimization_barrier(jnp.sum(weights, axis=1, keepdims=True))
        probs_low = probs.astype(jnp.bfloat16)
        head_out = jnp.dot(probs_low, value_columns, preferred_element_type=jnp.float32)
        out_parts.append(head_out.astype(jnp.bfloat16).reshape(STRETCH, GROUP * HEAD_SIZE))
        dprobs = jnp.dot(out_grads, value_columns.T, preferred_element_type=jnp.float32)
        row_delta = lax.optimization_barrier(jnp.sum(out_grads.astype(jnp.float32) * head_out, axis=1, keepdims=True))
        dscores = (probs * (dprobs - row_delta) * score_scale).astype(jnp.bfloat16)
        dq_parts.append(jnp.dot(dscores, key_cols, preferred_element_type=jnp.float32).reshape(STRETCH, GROUP * HEAD_SIZE))
        dk_parts.append(jnp.dot(dscores.T, query_rows, preferred_element_type=jnp.float32))
        dv_parts.append(jnp.dot(probs_low.T, out_grads, preferred_element_type=jnp.float32))
    return (jnp.concatenate(out_parts, axis=1), jnp.concatenate(dq_parts, axis=1), jnp.concatenate(dk_parts + dv_parts, axis=1))

def reference(noisy_q, noisy_k, noisy_value, clean_k, clean_value, q_gain, key_norm_gain, out_grad, window):
    q_norm, q_inv = normalize(noisy_q, q_gain)
    k_norm, k_inv = normalize(noisy_k, key_norm_gain)
    c_norm, c_inv = normalize(clean_k, key_norm_gain)
    noisy_kv = jnp.concatenate([k_norm, noisy_value], axis=1)
    clean_kv = jnp.concatenate([c_norm, clean_value], axis=1)
    kv_width = noisy_kv.shape[1]

    def stretch_step(clean_acc, stretch_id):
        begin_row = (stretch_id * STRETCH).astype(jnp.int32)
        q_rows = lax.dynamic_slice_in_dim(q_norm, begin_row, STRETCH, 0)
        grad_rows = lax.dynamic_slice_in_dim(out_grad, begin_row, STRETCH, 0)
        blocks = [lax.dynamic_slice_in_dim(noisy_kv, begin_row, STRETCH, 0)]
        mask_parts = [jnp.ones((STRETCH,), dtype=bool)]
        listed = window[stretch_id]
        starts = []
        flags = []
        for j in range(SLOTS):
            is_listed = listed[j] >= 0
            start_row = (jnp.maximum(listed[j], 0) * STRETCH).astype(jnp.int32)
            blocks.append(lax.dynamic_slice_in_dim(clean_kv, start_row, STRETCH, 0))
            mask_parts.append(jnp.broadcast_to(is_listed, (STRETCH,)))
            starts.append(start_row)
            flags.append(is_listed)
        out_rows, dq_rows, dkv_rows = stretch_attention(q_rows, grad_rows, jnp.concatenate(blocks, axis=0), jnp.concatenate(mask_parts, axis=0))
        for j in range(SLOTS):
            current = lax.dynamic_slice_in_dim(clean_acc, starts[j], STRETCH, 0)
            added = jnp.where(flags[j], dkv_rows[(1 + j) * STRETCH:(2 + j) * STRETCH], jnp.float32(0.0))
            clean_acc = lax.dynamic_update_slice_in_dim(clean_acc, current + added, starts[j], 0)
        return (clean_acc, (out_rows, dq_rows, dkv_rows[:STRETCH]))
    init_acc = jnp.zeros((NCH * STRETCH, kv_width), dtype=jnp.float32)
    clean_grad, (out_all, dq_all, noisy_grad) = lax.scan(stretch_step, init_acc, jnp.arange(NCH, dtype=jnp.int32))
    attn_out = out_all.reshape(NCH * STRETCH, HQ * HEAD_SIZE)
    dq_norm = dq_all.reshape(NCH * STRETCH, HQ * HEAD_SIZE)
    noisy_grad = noisy_grad.reshape(NCH * STRETCH, kv_width)
    key_columns = KEY_VALUE_HEADS * HEAD_SIZE
    grad_q = norm_grad(noisy_q, q_gain, q_inv, dq_norm)
    grad_k = norm_grad(noisy_k, key_norm_gain, k_inv, noisy_grad[:, :key_columns])
    grad_v = noisy_grad[:, key_columns:].astype(jnp.bfloat16)
    grad_clean_k = norm_grad(clean_k, key_norm_gain, c_inv, clean_grad[:, :key_columns])
    grad_clean_v = clean_grad[:, key_columns:].astype(jnp.bfloat16)
    return (attn_out, grad_q, grad_k, grad_v, grad_clean_k, grad_clean_v)
```

```python
import jax
import jax.numpy as jnp
from jax import lax
from jax.sharding import PartitionSpec as P

HEAD_SIZE = 128
KEY_VALUE_HEADS = 8
GROUP = 3
STRETCH = 520
WINDOW = 3
SLOTS = 2
HQ = 24


EPSILON = 1e-06
NEG_FILL = -1e30


def head_sums(parts):
    stacked = jnp.stack(parts, axis=0)
    count = lax.axis_size("head")
    spread = jnp.broadcast_to(stacked[None], (count,) + stacked.shape)
    return jnp.sum(lax.all_to_all(spread, "head", 0, 0), axis=0)


def stretch_shift(value, steps):
    count = lax.axis_size("seq")
    pairs = [(i, i + 2 * steps) for i in range(count) if 0 <= i + 2 * steps < count]
    return lax.ppermute(value, "seq", pairs)


def core_swap(value):
    count = lax.axis_size("seq")
    return lax.ppermute(value, "seq", [(i, i ^ 1) for i in range(count)])


def attend(q_norm, out_grad, every_key, key_mask, local_kv):
    rows_dev = q_norm.shape[0]
    score_scale = HEAD_SIZE ** (-0.5)
    per_block = next(
        (count for count in range(1, GROUP + 1) if GROUP % count == 0 and count * rows_dev >= 512),
        GROUP,
    )
    out_parts, dq_parts, dk_parts, dv_parts = ([], [], [], [])
    key_cols = every_key[:, 0:HEAD_SIZE]
    value_columns = every_key[:, local_kv * HEAD_SIZE : (local_kv + 1) * HEAD_SIZE]
    dk_total = jnp.zeros((every_key.shape[0], HEAD_SIZE), dtype=jnp.float32)
    dv_total = jnp.zeros((every_key.shape[0], HEAD_SIZE), dtype=jnp.float32)
    for block_tile in range(GROUP // per_block):
        first_col = (0 + block_tile * per_block) * HEAD_SIZE
        last_col = first_col + per_block * HEAD_SIZE
        query_rows = q_norm[:, first_col:last_col].reshape(rows_dev * per_block, HEAD_SIZE)
        out_grads = out_grad[:, first_col:last_col].reshape(rows_dev * per_block, HEAD_SIZE)
        scores = (
            lax.dot_general(
                query_rows, key_cols, (((1,), (1,)), ((), ())), preferred_element_type=jnp.float32
            )
            * score_scale
        )
        scores = jnp.where(key_mask[None, :], scores, NEG_FILL)
        row_max = jnp.max(scores, axis=1, keepdims=True)
        weights = jnp.exp(scores - row_max)
        probs = weights / jnp.sum(weights, axis=1, keepdims=True)
        probs_low = probs.astype(jnp.bfloat16)
        head_out = jnp.dot(probs_low, value_columns, preferred_element_type=jnp.float32)
        out_parts.append(head_out.astype(jnp.bfloat16).reshape(rows_dev, per_block * HEAD_SIZE))
        dprobs = lax.dot_general(
            out_grads, value_columns, (((1,), (1,)), ((), ())), preferred_element_type=jnp.float32
        )
        row_delta = jnp.sum(out_grads.astype(jnp.float32) * head_out, axis=1, keepdims=True)
        dscores = (probs * (dprobs - row_delta) * score_scale).astype(jnp.bfloat16)
        dq_parts.append(
            jnp.dot(dscores, key_cols, preferred_element_type=jnp.float32).reshape(
                rows_dev, per_block * HEAD_SIZE
            )
        )
        dk_total = dk_total + lax.dot_general(
            dscores, query_rows, (((0,), (0,)), ((), ())), preferred_element_type=jnp.float32
        )
        dv_total = dv_total + lax.dot_general(
            probs_low, out_grads, (((0,), (0,)), ((), ())), preferred_element_type=jnp.float32
        )
    dk_parts.append(dk_total)
    dv_parts.append(dv_total)
    return (
        jnp.concatenate(out_parts, axis=1),
        jnp.concatenate(dq_parts, axis=1),
        jnp.concatenate(dk_parts + dv_parts, axis=1),
    )


def on_device(
    noisy_q, noisy_k, noisy_value, clean_k, clean_value, q_gain, key_norm_gain, out_grad, window
):
    rows_dev = noisy_q.shape[0]
    local_kv = noisy_k.shape[1] // HEAD_SIZE
    stretch_span = STRETCH // rows_dev
    seq_pos = lax.axis_index("seq")
    stretch_id = seq_pos // stretch_span
    q_full = noisy_q.astype(jnp.float32)
    k_full = noisy_k.astype(jnp.float32)
    c_full = clean_k.astype(jnp.float32)
    totals = head_sums(
        (
            jnp.sum(q_full * q_full, axis=1),
            jnp.sum(k_full * k_full, axis=1),
            jnp.sum(c_full * c_full, axis=1),
        )
    )
    q_width = HQ * HEAD_SIZE
    key_width = KEY_VALUE_HEADS * HEAD_SIZE
    q_inv = lax.rsqrt(totals[0] / q_width + EPSILON)[:, None]
    k_inv = lax.rsqrt(totals[1] / key_width + EPSILON)[:, None]
    c_inv = lax.rsqrt(totals[2] / key_width + EPSILON)[:, None]
    q_norm = (q_full * q_inv * q_gain[None, :]).astype(jnp.bfloat16)
    k_norm = (k_full * k_inv * key_norm_gain[None, :]).astype(jnp.bfloat16)
    c_norm = (c_full * c_inv * key_norm_gain[None, :]).astype(jnp.bfloat16)
    noisy_kv = jnp.concatenate([k_norm, noisy_value], axis=1)
    clean_kv = jnp.concatenate([c_norm, clean_value], axis=1)
    row_hit = jnp.arange(window.shape[0], dtype=jnp.int32)[:, None] == stretch_id
    listed = jnp.sum(jnp.where(row_hit, window, 0), axis=0)
    use = [jnp.any((listed == stretch_id - back) & (listed >= 0)) for back in (1, 2, 3)]
    got = [stretch_shift(clean_kv, back) for back in (1, 2, 3)]
    other = jnp.where(use[1], got[1], got[2])
    mine = jnp.concatenate([noisy_kv, got[0], other], axis=0)
    theirs = core_swap(mine)
    rows3 = 3 * rows_dev
    part_mask = jnp.concatenate(
        [
            jnp.ones((rows_dev,), dtype=bool),
            jnp.broadcast_to(use[0], (rows_dev,)),
            jnp.broadcast_to(use[1] | use[2], (rows_dev,)),
        ]
    )
    attn_out, dq_norm, dkv_all = attend(
        q_norm,
        out_grad,
        jnp.concatenate([mine, theirs], axis=0),
        jnp.concatenate([part_mask, part_mask]),
        local_kv,
    )
    reduced = dkv_all[:rows3] + core_swap(dkv_all[rows3:].astype(jnp.bfloat16)).astype(jnp.float32)
    noisy_total = reduced[:rows_dev]
    back1 = jnp.where(use[0], reduced[rows_dev : 2 * rows_dev], 0.0).astype(jnp.bfloat16)
    dother = reduced[2 * rows_dev :]
    back2 = jnp.where(use[1], dother, 0.0).astype(jnp.bfloat16)
    back3 = jnp.where(use[2], dother, 0.0).astype(jnp.bfloat16)
    clean_total = (
        stretch_shift(back2, -2).astype(jnp.float32)
        + stretch_shift(back3, -3).astype(jnp.float32)
        + stretch_shift(back1, -1).astype(jnp.float32)
    )
    key_columns = local_kv * HEAD_SIZE
    q_scaled = dq_norm * q_gain[None, :]
    k_scaled = noisy_total[:, :key_columns] * key_norm_gain[None, :]
    c_scaled = clean_total[:, :key_columns] * key_norm_gain[None, :]
    inner_sum = head_sums(
        (
            jnp.sum(q_scaled * q_full, axis=1),
            jnp.sum(k_scaled * k_full, axis=1),
            jnp.sum(c_scaled * c_full, axis=1),
        )
    )
    grad_q = (
        q_inv * q_scaled - q_full * q_inv * q_inv * q_inv * (inner_sum[0] / q_width)[:, None]
    ).astype(jnp.bfloat16)
    grad_k = (
        k_inv * k_scaled - k_full * k_inv * k_inv * k_inv * (inner_sum[1] / key_width)[:, None]
    ).astype(jnp.bfloat16)
    grad_clean_k = (
        c_inv * c_scaled - c_full * c_inv * c_inv * c_inv * (inner_sum[2] / key_width)[:, None]
    ).astype(jnp.bfloat16)
    grad_v = noisy_total[:, key_columns:].astype(jnp.bfloat16)
    grad_clean_v = clean_total[:, key_columns:].astype(jnp.bfloat16)
    return (attn_out, grad_q, grad_k, grad_v, grad_clean_k, grad_clean_v)


def solution(mesh):
    placed = (
        P("seq", "head"),
        P("seq", "head"),
        P("seq", "head"),
        P("seq", "head"),
        P("seq", "head"),
        P("head"),
        P("head"),
        P("seq", "head"),
        P(),
    )
    return jax.shard_map(
        on_device,
        mesh=mesh,
        in_specs=placed,
        out_specs=(
            P("seq", "head"),
            P("seq", "head"),
            P("seq", "head"),
            P("seq", "head"),
            P("seq", "head"),
            P("seq", "head"),
        ),
        check_vma=False,
    )
```

```python
import math

import jax
import jax.numpy as jnp
from jax import lax
from jax.experimental import pallas as pl
from jax.experimental.pallas import tpu as pltpu
from jax.sharding import PartitionSpec as P

HEAD_SIZE = 128
KEY_VALUE_HEADS = 8
GROUP = 3
STRETCH = 520
HQ = 24
EPSILON = 1e-06
HIDDEN = -1e30

PAD = 16
LANES = 128
F32 = jnp.float32
BF16 = jnp.bfloat16
SCORE_SCALE = HEAD_SIZE ** (-0.5)
LOG2E = math.log2(math.e)


def up(count, unit):
    return -(-count // unit) * unit


def shape(dims, kind):
    return jax.ShapeDtypeStruct(dims, kind)


def kernel_call(body, outs, flops, scratch=(), smem_first=False, nargs=0):
    specs = [pl.BlockSpec(memory_space=pltpu.VMEM)] * nargs
    if smem_first:
        specs[0] = pl.BlockSpec(memory_space=pltpu.SMEM)
    size = sum(math.prod(o.shape) * o.dtype.itemsize for o in jax.tree.leaves(outs))
    return pl.pallas_call(
        body,
        out_shape=outs,
        in_specs=specs,
        out_specs=jax.tree.map(lambda o: pl.BlockSpec(memory_space=pltpu.VMEM), outs),
        scratch_shapes=list(scratch),
        compiler_params=pltpu.CompilerParams(vmem_limit_bytes=40 * 2**20),
        cost_estimate=pl.CostEstimate(flops=flops, bytes_accessed=2 * size, transcendentals=0),
    )


def dot(a, b, ca, cb):
    return lax.dot_general(a, b, (((ca,), (cb,)), ((), ())), preferred_element_type=F32)


def halves(x):
    high = x.astype(BF16)
    return high, (x - high.astype(F32)).astype(BF16)


def to_lanes(x, row):
    pick = (lax.broadcasted_iota(jnp.int32, (8, x.shape[1]), 0) == row).astype(BF16)
    high, low = halves(x)
    return dot(pick, high, 1, 1) + dot(pick, low, 1, 1)


def to_rows(x):
    row = lax.broadcasted_iota(jnp.int32, (8, 3 * LANES), 0)
    group = lax.broadcasted_iota(jnp.int32, (8, 3 * LANES), 1) // LANES
    pick = (row == group).astype(BF16)
    high, low = halves(x)
    rows = dot(high, pick, 0, 0) + dot(low, pick, 0, 0)
    return [rows[:, i * LANES : (i + 1) * LANES] for i in range(3)]


def added(ref):
    total = ref[0]
    for i in range(1, ref.shape[0]):
        total = total + ref[i]
    return total


def inverses(ref):
    sums = to_rows(added(ref))
    widths = (HQ * HEAD_SIZE, KEY_VALUE_HEADS * HEAD_SIZE, KEY_VALUE_HEADS * HEAD_SIZE)
    return [lax.rsqrt(s / w + EPSILON) for s, w in zip(sums, widths)]


def squares_body(q_ref, k_ref, c_ref, out_ref):
    rows = None
    for i, ref in enumerate((q_ref, k_ref, c_ref)):
        x = ref[...].astype(F32)
        part = to_lanes(x * x, i)
        rows = part if rows is None else rows + part
    for peer in range(out_ref.shape[0]):
        out_ref[peer] = rows


def keys_body(sums_ref, k_ref, v_ref, c_ref, cv_ref, gain_ref, noisy_ref, clean_ref, wide):
    _, k_inv, c_inv = inverses(sums_ref)
    rows = k_ref.shape[0]
    wide[...] = jnp.zeros_like(wide)
    wide[0:rows, 0:LANES] = c_ref[...].astype(F32) * c_inv * gain_ref[...]
    wide[0:rows, LANES:] = cv_ref[...].astype(F32)
    clean_ref[...] = wide[...].astype(BF16)
    wide[0:rows, 0:LANES] = k_ref[...].astype(F32) * k_inv * gain_ref[...]
    wide[0:rows, LANES:] = v_ref[...].astype(F32)
    noisy_ref[...] = wide[...].astype(BF16)


def queries_body(sums_ref, q_ref, g_ref, gain_ref, q_out, gt_out, wide):
    q_inv, _, _ = inverses(sums_ref)
    rows = q_ref.shape[0]
    slot = up(rows, PAD)
    wide[...] = jnp.zeros_like(wide)
    for h in range(GROUP):
        cols = slice(h * HEAD_SIZE, (h + 1) * HEAD_SIZE)
        gain = gain_ref[:, cols] * (SCORE_SCALE * LOG2E)
        wide[h * slot : h * slot + rows, :] = q_ref[:, cols].astype(F32) * q_inv * gain
    q_out[...] = wide[...].astype(BF16)
    for h in range(GROUP):
        cols = slice(h * HEAD_SIZE, (h + 1) * HEAD_SIZE)
        wide[h * slot : h * slot + rows, :] = g_ref[:, cols].astype(F32)
    gt_out[...] = wide[...].T.astype(BF16)


def attend_body(
    hide_ref, q_ref, gt_ref, n0, p0, o0, n1, p1, o1,
    out_ref, dq_ref, own_n, own_c, far_n, far_c, s_ref, e_ref,
):
    rows = out_ref.shape[0]
    slot = n0.shape[0]
    whole = rows // PAD * PAD
    blocks = (n0, p0, o0, n1, p1, o1)
    q = q_ref[...]
    top = None
    for j, ref in enumerate(blocks):
        s = dot(ref[:, :LANES], q, 1, 1)
        if j % 3:
            s = s + hide_ref[j % 3 - 1]
        tail = s[whole:]
        real = lax.broadcasted_iota(jnp.int32, tail.shape, 0) < rows - whole
        tail = jnp.where(real, tail, HIDDEN)
        s_ref[j, 0:whole] = s[:whole]
        s_ref[j, whole:slot] = tail
        here = jnp.maximum(
            jnp.max(s[:whole], axis=0, keepdims=True), jnp.max(tail, axis=0, keepdims=True)
        )
        top = here if top is None else jnp.maximum(top, here)
    total = None
    out_t = None
    for j, ref in enumerate(blocks):
        e = jnp.exp2(s_ref[j] - top)
        part = jnp.sum(e, axis=0, keepdims=True)
        low = e.astype(BF16)
        e_ref[j] = low
        share = dot(ref[:, LANES:], low, 0, 0)
        total = part if total is None else total + part
        out_t = share if out_t is None else out_t + share
    inv = 1.0 / total
    out_t = out_t * inv
    gt = gt_ref[...].astype(F32)
    delta = jnp.sum(gt * out_t, axis=0, keepdims=True) * inv
    gt = gt * inv
    g = gt.T.astype(BF16)
    gt = gt.astype(BF16)
    out = out_t.T
    for h in range(GROUP):
        out_ref[:, h * HEAD_SIZE : (h + 1) * HEAD_SIZE] = out[
            h * slot : h * slot + rows
        ].astype(BF16)
    dq_t = None
    for j, ref in enumerate(blocks):
        low = e_ref[j]
        dp = dot(ref[:, LANES:], gt, 1, 0)
        ds = (low.astype(F32) * (dp - delta)).astype(BF16)
        dv = dot(low, g, 1, 0)[:rows]
        dk = dot(ds, q, 1, 0)[:rows] * (1.0 / LOG2E)
        share = dot(ref[:, :LANES], ds, 0, 0)
        dq_t = share if dq_t is None else dq_t + share
        if j == 0:
            own_n[:, :LANES] = dk
            own_n[:, LANES:] = dv
        elif j < 3:
            own_c[j - 1, :, :LANES] = dk
            own_c[j - 1, :, LANES:] = dv
        elif j == 3:
            far_n[:, :LANES] = dk.astype(BF16)
            far_n[:, LANES:] = dv.astype(BF16)
        else:
            far_c[j - 4, :, :LANES] = dk.astype(BF16)
            far_c[j - 4, :, LANES:] = dv.astype(BF16)
    dq = dq_t.T * SCORE_SCALE
    for h in range(GROUP):
        dq_ref[:, h * HEAD_SIZE : (h + 1) * HEAD_SIZE] = dq[h * slot : h * slot + rows]


def join_body(use_ref, own_ref, far_ref, back1, back2, back3):
    prev = own_ref[0] + far_ref[0].astype(F32)
    other = own_ref[1] + far_ref[1].astype(F32)
    back1[...] = (prev * use_ref[0]).astype(BF16)
    back2[...] = (other * use_ref[1]).astype(BF16)
    back3[...] = (other * use_ref[2]).astype(BF16)


def key_totals(own_n, far_n, r1, r2, r3):
    noisy = own_n[...] + far_n[...].astype(F32)
    clean = r1[...].astype(F32) + r2[...].astype(F32) + r3[...].astype(F32)
    return noisy, clean


def inner_body(
    q_ref, k_ref, c_ref, q_gain, k_gain, dq_ref, own_n, far_n, r1, r2, r3, out_ref
):
    noisy, clean = key_totals(own_n, far_n, r1, r2, r3)
    rows = to_lanes(dq_ref[...] * q_gain[...] * q_ref[...].astype(F32), 0)
    rows = rows + to_lanes(noisy[:, :LANES] * k_gain[...] * k_ref[...].astype(F32), 1)
    rows = rows + to_lanes(clean[:, :LANES] * k_gain[...] * c_ref[...].astype(F32), 2)
    for peer in range(out_ref.shape[0]):
        out_ref[peer] = rows


def finish_body(
    sums_ref, inner_ref, q_ref, k_ref, c_ref, q_gain, k_gain, dq_ref, own_n, far_n, r1, r2, r3,
    grad_q, grad_k, grad_v, grad_ck, grad_cv,
):
    q_inv, k_inv, c_inv = inverses(sums_ref)
    q_sum, k_sum, c_sum = to_rows(added(inner_ref))
    noisy, clean = key_totals(own_n, far_n, r1, r2, r3)
    q_pull = q_inv * q_inv * q_inv * (q_sum / (HQ * HEAD_SIZE))
    for h in range(GROUP):
        cols = slice(h * HEAD_SIZE, (h + 1) * HEAD_SIZE)
        grad_q[:, cols] = (
            q_inv * (dq_ref[:, cols] * q_gain[:, cols]) - q_ref[:, cols].astype(F32) * q_pull
        ).astype(BF16)
    width = KEY_VALUE_HEADS * HEAD_SIZE
    for inv, total, mean, ref, out in (
        (k_inv, noisy, k_sum, k_ref, grad_k),
        (c_inv, clean, c_sum, c_ref, grad_ck),
    ):
        pull = inv * inv * inv * (mean / width)
        out[...] = (
            inv * (total[:, :LANES] * k_gain[...]) - ref[...].astype(F32) * pull
        ).astype(BF16)
    grad_v[...] = noisy[:, LANES:].astype(BF16)
    grad_cv[...] = clean[:, LANES:].astype(BF16)


def head_exchange(value):
    return lax.all_to_all(value, "head", 0, 0)


def stretch_shift(value, steps):
    count = lax.axis_size("seq")
    pairs = [(i, i + 2 * steps) for i in range(count) if 0 <= i + 2 * steps < count]
    return lax.ppermute(value, "seq", pairs)


def core_swap(value):
    count = lax.axis_size("seq")
    return lax.ppermute(value, "seq", [(i, i ^ 1) for i in range(count)])


def on_device(
    noisy_q, noisy_k, noisy_value, clean_k, clean_value, q_gain, key_norm_gain, out_grad, window
):
    rows = noisy_q.shape[0]
    slot = up(rows, PAD)
    stack = up(GROUP * slot, LANES)
    peers = lax.axis_size("head")
    stretch_id = lax.axis_index("seq") // 2
    row_hit = jnp.arange(window.shape[0], dtype=jnp.int32)[:, None] == stretch_id
    listed = jnp.sum(jnp.where(row_hit, window, 0), axis=0)
    back = stretch_id - jnp.arange(1, 4, dtype=jnp.int32)
    use = jnp.any((listed[None, :] == back[:, None]) & (back[:, None] >= 0), axis=1)
    use_f = use.astype(F32)
    hide = jnp.where(jnp.stack([use[0], use[1] | use[2]]), 0.0, HIDDEN).astype(F32)
    q_gain = q_gain[None, :]
    k_gain = key_norm_gain[None, :]

    sums = kernel_call(squares_body, shape((peers, 8, rows), F32), 10**6, nargs=3)(
        noisy_q, noisy_k, clean_k
    )
    sums = head_exchange(sums)
    pack = shape((slot, 2 * LANES), BF16)
    noisy_kv, clean_kv = kernel_call(
        keys_body, (pack, pack), 10**6, [pltpu.VMEM((slot, 2 * LANES), F32)], nargs=6
    )(sums, noisy_k, noisy_value, clean_k, clean_value, k_gain)
    got = [stretch_shift(clean_kv, steps) for steps in (1, 2, 3)]
    q_norm, g_turned = kernel_call(
        queries_body,
        (shape((stack, LANES), BF16), shape((LANES, stack), BF16)),
        10**6,
        [pltpu.VMEM((stack, LANES), F32)],
        nargs=4,
    )(sums, noisy_q, out_grad, q_gain)
    noisy_far = core_swap(noisy_kv)
    prev_far = core_swap(got[0])
    other = jnp.where(use[1], got[1], got[2])
    other_far = core_swap(other)
    grad_low = shape((rows, 2 * LANES), BF16)
    attn_out, dq, own_n, own_c, far_n, far_c = kernel_call(
        attend_body,
        (
            shape((rows, GROUP * LANES), BF16),
            shape((rows, GROUP * LANES), F32),
            shape((rows, 2 * LANES), F32),
            shape((2, rows, 2 * LANES), F32),
            grad_low,
            shape((2, rows, 2 * LANES), BF16),
        ),
        12 * rows * GROUP * 6 * slot * LANES,
        [pltpu.VMEM((6, slot, stack), F32), pltpu.VMEM((6, slot, stack), BF16)],
        smem_first=True,
        nargs=9,
    )(hide, q_norm, g_turned, noisy_kv, got[0], other, noisy_far, prev_far, other_far)
    clean_far = core_swap(far_c)
    back1, back2, back3 = kernel_call(
        join_body, (grad_low, grad_low, grad_low), 10**6, smem_first=True, nargs=3
    )(use_f, own_c, clean_far)
    r2 = stretch_shift(back2, -2)
    r3 = stretch_shift(back3, -3)
    r1 = stretch_shift(back1, -1)
    far_n = core_swap(far_n)
    inner = kernel_call(inner_body, shape((peers, 8, rows), F32), 10**6, nargs=11)(
        noisy_q, noisy_k, clean_k, q_gain, k_gain, dq, own_n, far_n, r1, r2, r3
    )
    inner = head_exchange(inner)
    key_grad = shape((rows, LANES), BF16)
    grad_q, grad_k, grad_v, grad_ck, grad_cv = kernel_call(
        finish_body,
        (shape((rows, GROUP * LANES), BF16), key_grad, key_grad, key_grad, key_grad),
        10**6,
        nargs=13,
    )(sums, inner, noisy_q, noisy_k, clean_k, q_gain, k_gain, dq, own_n, far_n, r1, r2, r3)
    return (attn_out, grad_q, grad_k, grad_v, grad_ck, grad_cv)


def solution(mesh):
    tokens = P("seq", "head")
    return jax.shard_map(
        on_device,
        mesh=mesh,
        in_specs=(tokens,) * 5 + (P("head"), P("head"), tokens, P()),
        out_specs=(tokens,) * 6,
        check_vma=False,
    )
```

```python
import math

import jax
import jax.numpy as jnp
from jax import lax
from jax.experimental import pallas as pl
from jax.experimental.pallas import tpu as pltpu
from jax.sharding import PartitionSpec as P

HEAD_SIZE = 128
KEY_VALUE_HEADS = 8
GROUP = 3
STRETCH = 520
HQ = 24
TOKENS = STRETCH // 2
EPSILON = 1e-06
HIDDEN = -1e30

PAD = 16
LANES = 128
F32 = jnp.float32
BF16 = jnp.bfloat16
SCORE_SCALE = HEAD_SIZE ** (-0.5)
LOG2E = math.log2(math.e)


def up(count, unit):
    return -(-count // unit) * unit


def shape(dims, kind):
    return jax.ShapeDtypeStruct(dims, kind)


def kernel_call(body, outs, flops, scratch=(), smem=(), nargs=0):
    specs = [pl.BlockSpec(memory_space=pltpu.SMEM if i in smem else pltpu.VMEM) for i in range(nargs)]
    size = sum(math.prod(o.shape) * o.dtype.itemsize for o in jax.tree.leaves(outs))
    return pl.pallas_call(
        body,
        out_shape=outs,
        in_specs=specs,
        out_specs=jax.tree.map(lambda o: pl.BlockSpec(memory_space=pltpu.VMEM), outs),
        scratch_shapes=list(scratch),
        compiler_params=pltpu.CompilerParams(vmem_limit_bytes=32 * 2**20),
        cost_estimate=pl.CostEstimate(flops=flops, bytes_accessed=size, transcendentals=0),
    )


def dot(a, b, ca, cb):
    return lax.dot_general(a, b, (((ca,), (cb,)), ((), ())), preferred_element_type=F32)


def halves(x):
    high = x.astype(BF16)
    return high, (x - high.astype(F32)).astype(BF16)


def to_lanes(x, row):
    pick = (lax.broadcasted_iota(jnp.int32, (8, x.shape[1]), 0) == row).astype(BF16)
    high, low = halves(x)
    return dot(pick, high, 1, 1) + dot(pick, low, 1, 1)


def to_rows(x):
    row = lax.broadcasted_iota(jnp.int32, (8, 3 * LANES), 0)
    group = lax.broadcasted_iota(jnp.int32, (8, 3 * LANES), 1) // LANES
    pick = (row == group).astype(BF16)
    high, low = halves(x)
    rows = dot(high, pick, 0, 0) + dot(low, pick, 0, 0)
    return [rows[:, i * LANES : (i + 1) * LANES] for i in range(3)]


def added(ref):
    total = ref[0]
    for i in range(1, ref.shape[0]):
        total = total + ref[i]
    return total


def inverses(ref):
    sums = to_rows(added(ref))
    widths = (HQ * HEAD_SIZE, KEY_VALUE_HEADS * HEAD_SIZE, KEY_VALUE_HEADS * HEAD_SIZE)
    return [lax.rsqrt(s / w + EPSILON) for s, w in zip(sums, widths)]


def squares_body(q_ref, k_ref, c_ref, out_ref):
    rows = None
    for i, ref in enumerate((q_ref, k_ref, c_ref)):
        x = ref[...].astype(F32)
        part = to_lanes(x * x, i)
        rows = part if rows is None else rows + part
    for peer in range(out_ref.shape[0]):
        out_ref[peer] = rows


def norms_body(
    sums_ref, q_ref, k_ref, c_ref, v_ref, cv_ref, g_ref, q_gain, k_gain,
    noisy_ref, clean_ref, out, wide, tall,
):
    q_inv, k_inv, c_inv = inverses(sums_ref)
    rows = k_ref.shape[0]
    slot = up(rows, PAD)
    wide[rows:] = jnp.zeros((slot - rows, 2 * LANES), F32)
    wide[0:rows, 0:LANES] = c_ref[...].astype(F32) * c_inv * k_gain[...]
    wide[0:rows, LANES:] = cv_ref[...].astype(F32)
    clean_ref[...] = wide[...].astype(BF16)
    wide[0:rows, 0:LANES] = k_ref[...].astype(F32) * k_inv * k_gain[...]
    wide[0:rows, LANES:] = v_ref[...].astype(F32)
    noisy_ref[...] = wide[...].astype(BF16)
    for h in range(2 * GROUP):
        tall[h * slot + rows : (h + 1) * slot] = jnp.zeros((slot - rows, LANES), F32)
    for h in range(GROUP):
        cols = slice(h * HEAD_SIZE, (h + 1) * HEAD_SIZE)
        gain = q_gain[:, cols] * (SCORE_SCALE * LOG2E)
        tall[h * slot : h * slot + rows, :] = q_ref[:, cols].astype(F32) * q_inv * gain
        at = (GROUP + h) * slot
        tall[at : at + rows, :] = g_ref[:, cols].astype(F32)
    out[...] = tall[...].astype(BF16)


def both(out, own, far, first, span):
    core = lax.axis_index("seq") % 2

    @pl.when(core == 0)
    def _():
        out[0:span] = own[first : first + span]
        out[span : 2 * span] = far[first : first + span]

    @pl.when(core == 1)
    def _():
        out[0:span] = far[first : first + span]
        out[span : 2 * span] = own[first : first + span]

    out[2 * span :] = jnp.zeros((out.shape[0] - 2 * span, out.shape[1]), out.dtype)


def listed(window_ref):
    here = lax.axis_index("seq") // 2
    found = []
    for steps in (1, 2, 3):
        at = here - steps
        hit = window_ref[here, 0] == at
        for j in range(1, window_ref.shape[1]):
            hit = hit | (window_ref[here, j] == at)
        found.append(hit & (at >= 0))
    return found


def scores(key_ref, q, rows):
    whole = rows // PAD * PAD
    s = dot(key_ref[:, :LANES], q, 1, 1)
    tail = s[whole:]
    real = lax.broadcasted_iota(jnp.int32, tail.shape, 0) < rows - whole
    return s[:whole], jnp.where(real, tail, HIDDEN)


def noisy_body(own, far, keys, q_out, gt_out, e_out, sum_out, stats, g_rows):
    span = own.shape[0] // 2
    both(q_out, own, far, 0, span)
    both(g_rows, own, far, span, span)
    gt = g_rows[...].astype(F32).T
    gt_out[...] = gt.astype(BF16)
    body, tail = scores(keys, q_out[...], TOKENS)
    whole = body.shape[0]
    top = jnp.maximum(
        jnp.max(body, axis=0, keepdims=True), jnp.max(tail, axis=0, keepdims=True)
    )
    body = jnp.exp2(body - top)
    tail = jnp.exp2(tail - top)
    total = jnp.sum(body, axis=0, keepdims=True) + jnp.sum(tail, axis=0, keepdims=True)
    e_out[0:whole] = body.astype(BF16)
    e_out[whole:] = tail.astype(BF16)
    sums = dot(keys[:, LANES:], e_out[...], 0, 0)
    sum_out[...] = sums
    stats[...] = jnp.zeros_like(stats)
    stats[0:1] = top
    stats[1:2] = total
    stats[2:3] = jnp.sum(gt * sums, axis=0, keepdims=True)


def clean_body(
    window_ref, got1, got2, got3, q_ref, gt_ref, noisy_stats, other, e_out, sum_out, stats, s_ref
):
    use1, use2, use3 = listed(window_ref)

    @pl.when(use2)
    def _():
        other[...] = got2[...]

    @pl.when(jnp.logical_not(use2))
    def _():
        other[...] = got3[...]

    q = q_ref[...]
    top = None
    for j, (ref, use) in enumerate(((got1, use1), (other, use2 | use3))):
        hide = jnp.where(use, 0.0, HIDDEN)
        body, tail = scores(ref, q, TOKENS)
        whole = body.shape[0]
        body = body + hide
        s_ref[j, 0:whole] = body
        s_ref[j, whole:] = tail
        here = jnp.maximum(
            jnp.max(body, axis=0, keepdims=True),
            jnp.max(tail + hide, axis=0, keepdims=True),
        )
        top = here if top is None else jnp.maximum(top, here)
        s_ref[j, whole:] = tail + hide
    total = None
    sums = None
    for j, ref in enumerate((got1, other)):
        e = jnp.exp2(s_ref[j] - top)
        part = jnp.sum(e, axis=0, keepdims=True)
        low = e.astype(BF16)
        e_out[j] = low
        share = dot(ref[:, LANES:], low, 0, 0)
        total = part if total is None else total + part
        sums = share if sums is None else sums + share
    sum_out[...] = sums
    stats[...] = noisy_stats[...]
    stats[3:4] = top
    stats[4:5] = total
    stats[5:6] = jnp.sum(gt_ref[...].astype(F32) * sums, axis=0, keepdims=True)


def key_grads(key_ref, e, gt, g, delta, q):
    dp = dot(key_ref[:, LANES:], gt, 1, 0)
    ds = (e.astype(F32) * (dp - delta)).astype(BF16)
    dv = dot(e, g, 1, 0)
    dk = dot(ds, q, 1, 0) * (1.0 / LOG2E)
    return ds, dk, dv


def clean_grad_body(
    window_ref, own, far, q_ref, gt_ref, got1, other, e_ref, back1, back2, back3, ds_out, merged
):
    use1, use2, use3 = listed(window_ref)
    groups = [(ref[i : i + 1], ref[i + 1 : i + 2], ref[i + 2 : i + 3])
              for ref in (own, far) for i in (0, 3)]
    top = groups[0][0]
    for group in groups[1:]:
        top = jnp.maximum(top, group[0])
    weights = [jnp.exp2(group[0] - top) for group in groups]
    inv = 1.0 / sum(w * group[1] for w, group in zip(weights, groups))
    delta = sum(w * group[2] for w, group in zip(weights, groups)) * inv
    noisy, clean = weights[0] * inv, weights[1] * inv
    merged[...] = jnp.zeros_like(merged)
    merged[0:1] = noisy
    merged[1:2] = clean
    merged[2:3] = delta * noisy
    gt = gt_ref[...].astype(F32) * clean
    g = gt.T.astype(BF16)
    gt = gt.astype(BF16)
    q = q_ref[...]
    rows = back1.shape[0]
    for j, (ref, outs) in enumerate(
        ((other, ((back2, use2), (back3, use3))), (got1, ((back1, use1),)))
    ):
        at = 1 - j
        ds, dk, dv = key_grads(ref, e_ref[at], gt, g, delta * clean, q)
        ds_out[at] = ds
        for out, use in outs:
            keep = jnp.where(use, 1.0, 0.0)
            out[:, :LANES] = (dk[:rows] * keep).astype(BF16)
            out[:, LANES:] = (dv[:rows] * keep).astype(BF16)


def noisy_grad_body(
    merged, q_ref, gt_ref, keys, got1, other, e_ref, ds_ref, noisy_sum, clean_sum,
    grads, own, far, wide,
):
    core = lax.axis_index("seq") % 2
    span = own.shape[0] // 2
    mine = pl.ds(pl.multiple_of(core * span, 8), span)
    theirs = pl.ds(pl.multiple_of((1 - core) * span, 8), span)
    noisy = merged[0:1]
    gt = gt_ref[...].astype(F32) * noisy
    g = gt.T.astype(BF16)
    ds, dk, dv = key_grads(keys, e_ref[...], gt.astype(BF16), g, merged[2:3], q_ref[...])
    rows = grads.shape[0]
    grads[:, :LANES] = dk[:rows]
    grads[:, LANES:] = dv[:rows]
    dq = dot(keys[:, :LANES], ds, 0, 0)
    dq = dq + dot(got1[:, :LANES], ds_ref[0], 0, 0)
    dq = dq + dot(other[:, :LANES], ds_ref[1], 0, 0)
    wide[0] = (noisy_sum[...] * noisy + clean_sum[...] * merged[1:2]).T
    wide[1] = (dq * SCORE_SCALE).T
    for i in range(2):
        own[i * span : (i + 1) * span] = wide[i, mine]
        far[i * span : (i + 1) * span] = wide[i, theirs].astype(BF16)


def clean_total_body(c_ref, k_ref, k_gain, grads, r1, r2, r3, sums, total_ref, grad_v, grad_cv):
    clean = r1[...].astype(F32) + r2[...].astype(F32) + r3[...].astype(F32)
    total_ref[...] = clean
    rows = to_lanes(clean[:, :LANES] * k_gain[...] * c_ref[...].astype(F32), 2)
    sums[...] = rows + to_lanes(grads[:, :LANES] * k_gain[...] * k_ref[...].astype(F32), 1)
    grad_v[...] = grads[:, LANES:].astype(BF16)
    grad_cv[...] = clean[:, LANES:].astype(BF16)


def inner_body(own, far, q_ref, q_gain, sums, attn_out, dq_out, out_ref):
    span = own.shape[0] // 2
    slot = span // GROUP
    rows = attn_out.shape[0]
    total = own[...] + far[...].astype(F32)
    for h in range(GROUP):
        cols = slice(h * HEAD_SIZE, (h + 1) * HEAD_SIZE)
        attn_out[:, cols] = total[h * slot : h * slot + rows].astype(BF16)
        at = span + h * slot
        dq_out[:, cols] = total[at : at + rows]
    part = sums[...] + to_lanes(dq_out[...] * q_gain[...] * q_ref[...].astype(F32), 0)
    for peer in range(out_ref.shape[0]):
        out_ref[peer] = part


def finish_body(
    sums_ref, inner_ref, q_ref, k_ref, c_ref, q_gain, k_gain, dq_ref, noisy_ref, clean_ref,
    grad_q, grad_k, grad_ck,
):
    q_inv, k_inv, c_inv = inverses(sums_ref)
    q_sum, k_sum, c_sum = to_rows(added(inner_ref))
    q_pull = q_inv * q_inv * q_inv * (q_sum / (HQ * HEAD_SIZE))
    for h in range(GROUP):
        cols = slice(h * HEAD_SIZE, (h + 1) * HEAD_SIZE)
        grad_q[:, cols] = (
            q_inv * (dq_ref[:, cols] * q_gain[:, cols]) - q_ref[:, cols].astype(F32) * q_pull
        ).astype(BF16)
    width = KEY_VALUE_HEADS * HEAD_SIZE
    for inv, total, mean, ref, out in (
        (k_inv, noisy_ref, k_sum, k_ref, grad_k),
        (c_inv, clean_ref, c_sum, c_ref, grad_ck),
    ):
        pull = inv * inv * inv * (mean / width)
        out[...] = (
            inv * (total[:, :LANES] * k_gain[...]) - ref[...].astype(F32) * pull
        ).astype(BF16)


def head_exchange(value):
    return lax.all_to_all(value, "head", 0, 0)


def stretch_shift(value, steps):
    count = lax.axis_size("seq")
    pairs = [(i, i + 2 * steps) for i in range(count) if 0 <= i + 2 * steps < count]
    return lax.ppermute(value, "seq", pairs)


def core_swap(value):
    count = lax.axis_size("seq")
    return lax.ppermute(value, "seq", [(i, i ^ 1) for i in range(count)])


def on_device(
    noisy_q, noisy_k, noisy_value, clean_k, clean_value, q_gain, key_norm_gain, out_grad, window
):
    rows = noisy_q.shape[0]
    slot = up(rows, PAD)
    span = GROUP * slot
    queries = up(2 * span, LANES)
    peers = lax.axis_size("head")
    q_gain = q_gain[None, :]
    k_gain = key_norm_gain[None, :]
    product = 2 * slot * queries * LANES
    stats = shape((8, queries), F32)
    turned = shape((LANES, queries), F32)

    fetched = (noisy_q, noisy_k, clean_k)
    sums = pl.pallas_call(
        squares_body,
        grid=(1,),
        out_shape=shape((peers, 8, rows), F32),
        in_specs=[pl.BlockSpec(a.shape, lambda i: (0, 0)) for a in fetched],
        out_specs=pl.BlockSpec((peers, 8, rows), lambda i: (0, 0, 0)),
        compiler_params=pltpu.CompilerParams(vmem_limit_bytes=60 * 2**20),
        cost_estimate=pl.CostEstimate(flops=10**10, bytes_accessed=10**6, transcendentals=0),
    )(*fetched)
    sums = head_exchange(sums)
    pack = shape((slot, 2 * LANES), BF16)
    noisy_kv, clean_kv, own = kernel_call(
        norms_body,
        (pack, pack, shape((2 * span, LANES), BF16)),
        10**6,
        [pltpu.VMEM((slot, 2 * LANES), F32), pltpu.VMEM((2 * span, LANES), F32)],
        nargs=9,
    )(sums, noisy_q, noisy_k, clean_k, noisy_value, clean_value, out_grad, q_gain, k_gain)
    got = [stretch_shift(clean_kv, steps) for steps in (1, 2, 3)]
    far = core_swap(own)
    q_all, g_turned, noisy_e, noisy_sum, noisy_stats = kernel_call(
        noisy_body,
        (
            shape((queries, LANES), BF16),
            shape((LANES, queries), BF16),
            shape((slot, queries), BF16),
            turned,
            stats,
        ),
        4 * product,
        [pltpu.VMEM((queries, LANES), BF16)],
        nargs=3,
    )(own, far, noisy_kv)
    pair = shape((2, slot, queries), BF16)
    other, clean_e, clean_sum, own_stats = kernel_call(
        clean_body,
        (pack, pair, turned, stats),
        8 * product,
        [pltpu.VMEM((2, slot, queries), F32)],
        smem=(0,),
        nargs=7,
    )(window, *got, q_all, g_turned, noisy_stats)
    far_stats = core_swap(own_stats)
    grad_low = shape((rows, 2 * LANES), BF16)
    back1, back2, back3, clean_ds, merged = kernel_call(
        clean_grad_body,
        (grad_low, grad_low, grad_low, pair, stats),
        8 * product,
        smem=(0,),
        nargs=8,
    )(window, own_stats, far_stats, q_all, g_turned, got[0], other, clean_e)
    r2 = stretch_shift(back2, -2)
    r3 = stretch_shift(back3, -3)
    r1 = stretch_shift(back1, -1)
    noisy_grads, own, far = kernel_call(
        noisy_grad_body,
        (
            shape((rows, 2 * LANES), F32),
            shape((2 * span, LANES), F32),
            shape((2 * span, LANES), BF16),
        ),
        8 * product,
        [pltpu.VMEM((2, queries, LANES), F32)],
        nargs=10,
    )(
        merged, q_all, g_turned, noisy_kv, got[0], other, noisy_e, clean_ds, noisy_sum, clean_sum
    )
    far = core_swap(far)
    key_grad = shape((rows, LANES), BF16)
    query_grad = shape((rows, GROUP * LANES), BF16)
    inner, clean_grads, grad_v, grad_cv = kernel_call(
        clean_total_body,
        (shape((8, rows), F32), shape((rows, 2 * LANES), F32), key_grad, key_grad),
        10**10,
        nargs=7,
    )(clean_k, noisy_k, k_gain, noisy_grads, r1, r2, r3)
    attn_out, dq, inner = kernel_call(
        inner_body,
        (query_grad, shape((rows, GROUP * LANES), F32), shape((peers, 8, rows), F32)),
        10**6,
        nargs=5,
    )(own, far, noisy_q, q_gain, inner)
    inner = head_exchange(inner)
    grad_q, grad_k, grad_ck = kernel_call(
        finish_body, (query_grad, key_grad, key_grad), 10**6, nargs=10
    )(sums, inner, noisy_q, noisy_k, clean_k, q_gain, k_gain, dq, noisy_grads, clean_grads)
    return (attn_out, grad_q, grad_k, grad_v, grad_ck, grad_cv)


def solution(mesh):
    tokens = P("seq", "head")
    return jax.shard_map(
        on_device,
        mesh=mesh,
        in_specs=(tokens,) * 5 + (P("head"), P("head"), tokens, P()),
        out_specs=(tokens,) * 6,
        check_vma=False,
    )
```

```python
import math

import jax
import jax.numpy as jnp
from jax import lax
from jax.experimental import pallas as pl
from jax.experimental.pallas import tpu as pltpu
from jax.sharding import PartitionSpec as P

HEAD_SIZE = 128
KEY_VALUE_HEADS = 8
GROUP = 3
STRETCH = 520
HQ = 24
TOKENS = STRETCH // 2
EPSILON = 1e-06
HIDDEN = -1e30

PAD = 16
LANES = 128
F32 = jnp.float32
BF16 = jnp.bfloat16
SCORE_SCALE = HEAD_SIZE ** (-0.5)
LOG2E = math.log2(math.e)


def up(count, unit):
    return -(-count // unit) * unit


def shape(dims, kind):
    return jax.ShapeDtypeStruct(dims, kind)


def kernel_call(body, outs, flops, scratch=(), smem=(), nargs=0):
    specs = [pl.BlockSpec(memory_space=pltpu.SMEM if i in smem else pltpu.VMEM) for i in range(nargs)]
    size = sum(math.prod(o.shape) * o.dtype.itemsize for o in jax.tree.leaves(outs))
    return pl.pallas_call(
        body,
        out_shape=outs,
        in_specs=specs,
        out_specs=jax.tree.map(lambda o: pl.BlockSpec(memory_space=pltpu.VMEM), outs),
        scratch_shapes=list(scratch),
        compiler_params=pltpu.CompilerParams(vmem_limit_bytes=32 * 2**20),
        cost_estimate=pl.CostEstimate(flops=flops, bytes_accessed=size, transcendentals=0),
    )


def dot(a, b, ca, cb):
    return lax.dot_general(a, b, (((ca,), (cb,)), ((), ())), preferred_element_type=F32)


def halves(x):
    high = x.astype(BF16)
    return high, (x - high.astype(F32)).astype(BF16)


def to_lanes(x, row):
    pick = (lax.broadcasted_iota(jnp.int32, (8, x.shape[1]), 0) == row).astype(BF16)
    high, low = halves(x)
    return dot(pick, high, 1, 1) + dot(pick, low, 1, 1)


def to_rows(x):
    row = lax.broadcasted_iota(jnp.int32, (3, 3 * LANES), 0)
    group = lax.broadcasted_iota(jnp.int32, (3, 3 * LANES), 1) // LANES
    pick = (row == group).astype(BF16)
    high, low = halves(x)
    rows = dot(high, pick, 0, 0) + dot(low, pick, 0, 0)
    return [rows[:, i * LANES : (i + 1) * LANES] for i in range(3)]


def added(ref):
    total = ref[0]
    for i in range(1, ref.shape[0]):
        total = total + ref[i]
    return total


def inverses(ref):
    sums = to_rows(added(ref))
    widths = (HQ * HEAD_SIZE, KEY_VALUE_HEADS * HEAD_SIZE, KEY_VALUE_HEADS * HEAD_SIZE)
    return [lax.rsqrt(s / w + EPSILON) for s, w in zip(sums, widths)]


def squares_body(q_ref, k_ref, c_ref, out_ref):
    rows = None
    for i, ref in enumerate((q_ref, k_ref, c_ref)):
        x = ref[...].astype(F32)
        part = to_lanes(x * x, i)
        rows = part if rows is None else rows + part
    for peer in range(out_ref.shape[0]):
        out_ref[peer] = rows[:3]


def norms_body(
    sums_ref, q_ref, k_ref, c_ref, v_ref, cv_ref, g_ref, q_gain, k_gain,
    noisy_ref, clean_ref, out, wide, tall,
):
    q_inv, k_inv, c_inv = inverses(sums_ref)
    rows = k_ref.shape[0]
    slot = up(rows, PAD)
    wide[rows:] = jnp.zeros((slot - rows, 2 * LANES), F32)
    wide[0:rows, 0:LANES] = c_ref[...].astype(F32) * c_inv * k_gain[...]
    wide[0:rows, LANES:] = cv_ref[...].astype(F32)
    clean_ref[...] = wide[...].astype(BF16)
    wide[0:rows, 0:LANES] = k_ref[...].astype(F32) * k_inv * k_gain[...]
    wide[0:rows, LANES:] = v_ref[...].astype(F32)
    noisy_ref[...] = wide[...].astype(BF16)
    for h in range(2 * GROUP):
        tall[h * slot + rows : (h + 1) * slot] = jnp.zeros((slot - rows, LANES), F32)
    for h in range(GROUP):
        cols = slice(h * HEAD_SIZE, (h + 1) * HEAD_SIZE)
        gain = q_gain[:, cols] * (SCORE_SCALE * LOG2E)
        tall[h * slot : h * slot + rows, :] = q_ref[:, cols].astype(F32) * q_inv * gain
        at = (GROUP + h) * slot
        tall[at : at + rows, :] = g_ref[:, cols].astype(F32)
    out[...] = tall[...].astype(BF16)


def both(out, own, far, first, span):
    core = lax.axis_index("seq") % 2

    @pl.when(core == 0)
    def _():
        out[0:span] = own[first : first + span]
        out[span : 2 * span] = far[first : first + span]

    @pl.when(core == 1)
    def _():
        out[0:span] = far[first : first + span]
        out[span : 2 * span] = own[first : first + span]

    out[2 * span :] = jnp.zeros((out.shape[0] - 2 * span, out.shape[1]), out.dtype)


def listed(window_ref):
    here = lax.axis_index("seq") // 2
    found = []
    for steps in (1, 2, 3):
        at = here - steps
        hit = window_ref[here, 0] == at
        for j in range(1, window_ref.shape[1]):
            hit = hit | (window_ref[here, j] == at)
        found.append(hit & (at >= 0))
    return found


def scores(key_ref, q, rows):
    whole = rows // PAD * PAD
    s = dot(key_ref[:, :LANES], q, 1, 1)
    tail = s[whole:]
    real = lax.broadcasted_iota(jnp.int32, tail.shape, 0) < rows - whole
    return s[:whole], jnp.where(real, tail, HIDDEN)


def noisy_body(own, far, keys, q_out, gt_out, e_out, sum_out, stats, g_rows):
    span = own.shape[0] // 2
    both(q_out, own, far, 0, span)
    both(g_rows, own, far, span, span)
    gt = g_rows[...].astype(F32).T
    gt_out[...] = gt.astype(BF16)
    body, tail = scores(keys, q_out[...], TOKENS)
    whole = body.shape[0]
    top = jnp.maximum(
        jnp.max(body, axis=0, keepdims=True), jnp.max(tail, axis=0, keepdims=True)
    )
    body = jnp.exp2(body - top)
    tail = jnp.exp2(tail - top)
    total = jnp.sum(body, axis=0, keepdims=True) + jnp.sum(tail, axis=0, keepdims=True)
    e_out[0:whole] = body.astype(BF16)
    e_out[whole:] = tail.astype(BF16)
    sums = dot(keys[:, LANES:], e_out[...], 0, 0)
    sum_out[...] = sums
    stats[...] = jnp.zeros_like(stats)
    stats[0:1] = top
    stats[1:2] = total
    stats[2:3] = jnp.sum(gt * sums, axis=0, keepdims=True)


def pair_body(own, far, out):
    out[0] = own[...]
    out[1] = far[...]


def clean_body(
    window_ref, near, far, q_ref, gt_ref, noisy_stats, keys, e_out, sum_out, stats, s_ref
):
    use1, use2, use3 = listed(window_ref)
    first = lax.axis_index("seq") % 2 == 0
    from_far = jnp.logical_not(first) & use2

    @pl.when(from_far)
    def _():
        keys[...] = far[...]

    @pl.when(jnp.logical_not(from_far))
    def _():
        keys[...] = near[...]

    hide = jnp.where(jnp.where(first, use1, use2 | use3), 0.0, HIDDEN)
    q = q_ref[...]
    top = None
    for j in range(2):
        body, tail = scores(keys.at[j], q, TOKENS)
        whole = body.shape[0]
        body = body + hide
        tail = tail + hide
        s_ref[j, 0:whole] = body
        s_ref[j, whole:] = tail
        here = jnp.maximum(
            jnp.max(body, axis=0, keepdims=True), jnp.max(tail, axis=0, keepdims=True)
        )
        top = here if top is None else jnp.maximum(top, here)
    total = None
    sums = None
    for j in range(2):
        e = jnp.exp2(s_ref[j] - top)
        part = jnp.sum(e, axis=0, keepdims=True)
        low = e.astype(BF16)
        e_out[j] = low
        share = dot(keys[j, :, LANES:], low, 0, 0)
        total = part if total is None else total + part
        sums = share if sums is None else sums + share
    sum_out[...] = sums
    stats[...] = noisy_stats[...]
    stats[3:4] = top
    stats[4:5] = total
    stats[5:6] = jnp.sum(gt_ref[...].astype(F32) * sums, axis=0, keepdims=True)


def key_grads(key_ref, e, gt, g, delta, q):
    dp = dot(key_ref[:, LANES:], gt, 1, 0)
    ds = (e.astype(F32) * (dp - delta)).astype(BF16)
    dv = dot(e, g, 1, 0)
    dk = dot(ds, q, 1, 0) * (1.0 / LOG2E)
    return ds, dk, dv


def clean_grad_body(
    window_ref, own, far, q_ref, gt_ref, keys, e_ref, near_out, far_out, ds_out, merged
):
    use1, use2, use3 = listed(window_ref)
    first = lax.axis_index("seq") % 2 == 0
    groups = [(ref[i : i + 1], ref[i + 1 : i + 2], ref[i + 2 : i + 3])
              for ref in (own, far) for i in (0, 3)]
    top = groups[0][0]
    for group in groups[1:]:
        top = jnp.maximum(top, group[0])
    weights = [jnp.exp2(group[0] - top) for group in groups]
    inv = 1.0 / sum(w * group[1] for w, group in zip(weights, groups))
    delta = sum(w * group[2] for w, group in zip(weights, groups)) * inv
    noisy, clean = weights[0] * inv, weights[1] * inv
    merged[...] = jnp.zeros_like(merged)
    merged[0:1] = noisy
    merged[1:2] = clean
    merged[2:3] = delta * noisy
    gt = gt_ref[...].astype(F32) * clean
    g = gt.T.astype(BF16)
    gt = gt.astype(BF16)
    q = q_ref[...]
    rows = near_out.shape[1]
    keep_near = jnp.where(jnp.where(first, use1, use3), 1.0, 0.0)
    keep_far = jnp.where(use2, 1.0, 0.0)
    for j in range(2):
        ds, dk, dv = key_grads(keys.at[j], e_ref[j], gt, g, delta * clean, q)
        ds_out[j] = ds
        for out, keep in ((near_out, keep_near), (far_out, keep_far)):
            out[j, :, :LANES] = (dk[:rows] * keep).astype(BF16)
            out[j, :, LANES:] = (dv[:rows] * keep).astype(BF16)


def noisy_grad_body(
    merged, q_ref, gt_ref, keys, clean_keys, e_ref, ds_ref, noisy_sum, clean_sum,
    grads, own, far, wide,
):
    core = lax.axis_index("seq") % 2
    span = own.shape[0] // 2
    mine = pl.ds(pl.multiple_of(core * span, 8), span)
    theirs = pl.ds(pl.multiple_of((1 - core) * span, 8), span)
    noisy = merged[0:1]
    gt = gt_ref[...].astype(F32) * noisy
    g = gt.T.astype(BF16)
    ds, dk, dv = key_grads(keys, e_ref[...], gt.astype(BF16), g, merged[2:3], q_ref[...])
    rows = grads.shape[0]
    grads[:, :LANES] = dk[:rows]
    grads[:, LANES:] = dv[:rows]
    dq = dot(keys[:, :LANES], ds, 0, 0)
    for j in range(2):
        dq = dq + dot(clean_keys[j, :, :LANES], ds_ref[j], 0, 0)
    wide[0] = (noisy_sum[...] * noisy + clean_sum[...] * merged[1:2]).T
    wide[1] = (dq * SCORE_SCALE).T
    for i in range(2):
        own[i * span : (i + 1) * span] = wide[i, mine]
        far[i * span : (i + 1) * span] = wide[i, theirs].astype(BF16)


def join_body(far, near, own_out, far_out):
    own_out[...] = near[0].astype(F32) + far[0].astype(F32)
    far_out[...] = (near[1].astype(F32) + far[1].astype(F32)).astype(BF16)


def inner_body(
    own, far, own_clean, far_clean, grads, q_ref, k_ref, c_ref, q_gain, k_gain,
    attn_out, dq_out, clean_out, grad_v, grad_cv, out_ref,
):
    clean = own_clean[...] + far_clean[...].astype(F32)
    clean_out[...] = clean
    grad_cv[...] = clean[:, LANES:].astype(BF16)
    grad_v[...] = grads[:, LANES:].astype(BF16)
    part = to_lanes(clean[:, :LANES] * k_gain[...] * c_ref[...].astype(F32), 2)
    part = part + to_lanes(grads[:, :LANES] * k_gain[...] * k_ref[...].astype(F32), 1)
    span = own.shape[0] // 2
    slot = span // GROUP
    rows = attn_out.shape[0]
    total = own[...] + far[...].astype(F32)
    for h in range(GROUP):
        cols = slice(h * HEAD_SIZE, (h + 1) * HEAD_SIZE)
        attn_out[:, cols] = total[h * slot : h * slot + rows].astype(BF16)
        at = span + h * slot
        dq_out[:, cols] = total[at : at + rows]
    part = part + to_lanes(dq_out[...] * q_gain[...] * q_ref[...].astype(F32), 0)
    for peer in range(out_ref.shape[0]):
        out_ref[peer] = part[:3]


def finish_body(
    sums_ref, inner_ref, q_ref, k_ref, c_ref, q_gain, k_gain, dq_ref, noisy_ref, clean_ref,
    grad_q, grad_k, grad_ck,
):
    q_inv, k_inv, c_inv = inverses(sums_ref)
    q_sum, k_sum, c_sum = to_rows(added(inner_ref))
    q_pull = q_inv * q_inv * q_inv * (q_sum / (HQ * HEAD_SIZE))
    for h in range(GROUP):
        cols = slice(h * HEAD_SIZE, (h + 1) * HEAD_SIZE)
        grad_q[:, cols] = (
            q_inv * (dq_ref[:, cols] * q_gain[:, cols]) - q_ref[:, cols].astype(F32) * q_pull
        ).astype(BF16)
    width = KEY_VALUE_HEADS * HEAD_SIZE
    for inv, total, mean, ref, out in (
        (k_inv, noisy_ref, k_sum, k_ref, grad_k),
        (c_inv, clean_ref, c_sum, c_ref, grad_ck),
    ):
        pull = inv * inv * inv * (mean / width)
        out[...] = (
            inv * (total[:, :LANES] * k_gain[...]) - ref[...].astype(F32) * pull
        ).astype(BF16)


def head_exchange(value):
    return lax.all_to_all(value, "head", 0, 0)


def stretch_shift(value, steps, far):
    count = lax.axis_size("seq")
    pairs = []
    for i in range(count):
        if far and i % 2 == 0:
            continue
        length = 2 if far else (1, 3)[i % 2]
        target = i + 2 * length * steps
        if 0 <= target < count:
            pairs.append((i, target))
    return lax.ppermute(value, "seq", pairs)


def core_swap(value):
    count = lax.axis_size("seq")
    return lax.ppermute(value, "seq", [(i, i ^ 1) for i in range(count)])


def on_device(
    noisy_q, noisy_k, noisy_value, clean_k, clean_value, q_gain, key_norm_gain, out_grad, window
):
    rows = noisy_q.shape[0]
    slot = up(rows, PAD)
    span = GROUP * slot
    queries = up(2 * span, LANES)
    peers = lax.axis_size("head")
    q_gain = q_gain[None, :]
    k_gain = key_norm_gain[None, :]
    product = 2 * slot * queries * LANES
    stats = shape((8, queries), F32)
    turned = shape((LANES, queries), F32)

    fetched = (noisy_q, noisy_k, clean_k)
    sums = pl.pallas_call(
        squares_body,
        grid=(1,),
        out_shape=shape((peers, 3, rows), F32),
        in_specs=[pl.BlockSpec(a.shape, lambda i: (0, 0)) for a in fetched],
        out_specs=pl.BlockSpec((peers, 3, rows), lambda i: (0, 0, 0)),
        compiler_params=pltpu.CompilerParams(vmem_limit_bytes=60 * 2**20),
        cost_estimate=pl.CostEstimate(flops=10**10, bytes_accessed=10**6, transcendentals=0),
    )(*fetched)
    sums = head_exchange(sums)
    pack = shape((slot, 2 * LANES), BF16)
    noisy_kv, clean_kv, own = kernel_call(
        norms_body,
        (pack, pack, shape((2 * span, LANES), BF16)),
        10**6,
        [pltpu.VMEM((slot, 2 * LANES), F32), pltpu.VMEM((2 * span, LANES), F32)],
        nargs=9,
    )(sums, noisy_q, noisy_k, clean_k, noisy_value, clean_value, out_grad, q_gain, k_gain)
    pair_kv = shape((2, slot, 2 * LANES), BF16)
    clean_kv = kernel_call(pair_body, pair_kv, 10**6, nargs=2)(clean_kv, core_swap(clean_kv))
    near_kv = stretch_shift(clean_kv, 1, False)
    far_kv = stretch_shift(clean_kv, 1, True)
    far = core_swap(own)
    q_all, g_turned, noisy_e, noisy_sum, noisy_stats = kernel_call(
        noisy_body,
        (
            shape((queries, LANES), BF16),
            shape((LANES, queries), BF16),
            shape((slot, queries), BF16),
            turned,
            stats,
        ),
        4 * product,
        [pltpu.VMEM((queries, LANES), BF16)],
        nargs=3,
    )(own, far, noisy_kv)
    pair = shape((2, slot, queries), BF16)
    keys, clean_e, clean_sum, own_stats = kernel_call(
        clean_body,
        (pair_kv, pair, turned, stats),
        8 * product,
        [pltpu.VMEM((2, slot, queries), F32)],
        smem=(0,),
        nargs=6,
    )(window, near_kv, far_kv, q_all, g_turned, noisy_stats)
    far_stats = core_swap(own_stats)
    pair_grad = shape((2, rows, 2 * LANES), BF16)
    near_back, far_back, clean_ds, merged = kernel_call(
        clean_grad_body,
        (pair_grad, pair_grad, pair, stats),
        8 * product,
        smem=(0,),
        nargs=7,
    )(window, own_stats, far_stats, q_all, g_turned, keys, clean_e)
    far_back = stretch_shift(far_back, -1, True)
    near_back = stretch_shift(near_back, -1, False)
    noisy_grads, own, far = kernel_call(
        noisy_grad_body,
        (
            shape((rows, 2 * LANES), F32),
            shape((2 * span, LANES), F32),
            shape((2 * span, LANES), BF16),
        ),
        8 * product,
        [pltpu.VMEM((2, queries, LANES), F32)],
        nargs=9,
    )(merged, q_all, g_turned, noisy_kv, keys, noisy_e, clean_ds, noisy_sum, clean_sum)
    far = core_swap(far)
    key_grad = shape((rows, LANES), BF16)
    query_grad = shape((rows, GROUP * LANES), BF16)
    own_clean, far_clean = kernel_call(
        join_body,
        (shape((rows, 2 * LANES), F32), shape((rows, 2 * LANES), BF16)),
        10**10,
        nargs=2,
    )(far_back, near_back)
    far_clean = core_swap(far_clean)
    attn_out, dq, clean_grads, grad_v, grad_cv, inner = kernel_call(
        inner_body,
        (
            query_grad,
            shape((rows, GROUP * LANES), F32),
            shape((rows, 2 * LANES), F32),
            key_grad,
            key_grad,
            shape((peers, 3, rows), F32),
        ),
        10**6,
        nargs=10,
    )(
        own, far, own_clean, far_clean, noisy_grads, noisy_q, noisy_k, clean_k, q_gain, k_gain
    )
    inner = head_exchange(inner)
    grad_q, grad_k, grad_ck = kernel_call(
        finish_body, (query_grad, key_grad, key_grad), 10**6, nargs=10
    )(sums, inner, noisy_q, noisy_k, clean_k, q_gain, k_gain, dq, noisy_grads, clean_grads)
    return (attn_out, grad_q, grad_k, grad_v, grad_ck, grad_cv)


def solution(mesh):
    tokens = P("seq", "head")
    return jax.shard_map(
        on_device,
        mesh=mesh,
        in_specs=(tokens,) * 5 + (P("head"), P("head"), tokens, P()),
        out_specs=(tokens,) * 6,
        check_vma=False,
    )
```

```python
import math

import jax
import jax.numpy as jnp
from jax import lax
from jax.experimental import pallas as pl
from jax.experimental.pallas import tpu as pltpu
from jax.sharding import PartitionSpec as P

HEAD_SIZE = 128
KEY_VALUE_HEADS = 8
GROUP = 3
STRETCH = 520
HQ = 24
TOKENS = STRETCH // 2
EPSILON = 1e-06
HIDDEN = -1e30

PAD = 16
LANES = 128
F32 = jnp.float32
BF16 = jnp.bfloat16
SCORE_SCALE = HEAD_SIZE ** (-0.5)
LOG2E = math.log2(math.e)


def up(count, unit):
    return -(-count // unit) * unit


def shape(dims, kind):
    return jax.ShapeDtypeStruct(dims, kind)


def kernel_call(body, outs, flops, scratch=(), smem=(), nargs=0):
    specs = [pl.BlockSpec(memory_space=pltpu.SMEM if i in smem else pltpu.VMEM) for i in range(nargs)]
    size = sum(math.prod(o.shape) * o.dtype.itemsize for o in jax.tree.leaves(outs))
    return pl.pallas_call(
        body,
        out_shape=outs,
        in_specs=specs,
        out_specs=jax.tree.map(lambda o: pl.BlockSpec(memory_space=pltpu.VMEM), outs),
        scratch_shapes=list(scratch),
        compiler_params=pltpu.CompilerParams(vmem_limit_bytes=32 * 2**20),
        cost_estimate=pl.CostEstimate(flops=flops, bytes_accessed=size, transcendentals=0),
    )


def dot(a, b, ca, cb):
    return lax.dot_general(a, b, (((ca,), (cb,)), ((), ())), preferred_element_type=F32)


def halves(x):
    high = x.astype(BF16)
    return high, (x - high.astype(F32)).astype(BF16)


def to_lanes(x, row):
    pick = (lax.broadcasted_iota(jnp.int32, (8, x.shape[1]), 0) == row).astype(BF16)
    high, low = halves(x)
    return dot(pick, high, 1, 1) + dot(pick, low, 1, 1)


def to_rows(x):
    count = x.shape[0]
    row = lax.broadcasted_iota(jnp.int32, (count, count * LANES), 0)
    group = lax.broadcasted_iota(jnp.int32, (count, count * LANES), 1) // LANES
    pick = (row == group).astype(BF16)
    high, low = halves(x)
    rows = dot(high, pick, 0, 0) + dot(low, pick, 0, 0)
    return [rows[:, i * LANES : (i + 1) * LANES] for i in range(count)]


def added(ref):
    total = ref[0]
    for i in range(1, ref.shape[0]):
        total = total + ref[i]
    return total


def inverse(sums, heads):
    return lax.rsqrt(sums / (heads * HEAD_SIZE) + EPSILON)


def pack_body(q_ref, g_ref, c_ref, v_ref, out, wide):
    rows = c_ref.shape[0]
    slot = up(rows, PAD)
    wide[0:rows, :LANES] = c_ref[...].astype(F32)
    wide[0:rows, LANES:] = v_ref[...].astype(F32)
    wide[rows:slot] = jnp.zeros((slot - rows, 2 * LANES), F32)
    for h in range(GROUP):
        cols = slice(h * HEAD_SIZE, (h + 1) * HEAD_SIZE)
        at = (1 + h) * slot
        wide[at : at + rows, :LANES] = q_ref[:, cols].astype(F32)
        wide[at : at + rows, LANES:] = g_ref[:, cols].astype(F32)
        wide[at + rows : at + slot] = jnp.zeros((slot - rows, 2 * LANES), F32)
    out[...] = wide[...].astype(BF16)


def pair_body(own, far, out):
    out[0] = own[...]
    out[1] = far[...]


def squares_body(own, far, k_ref, out_ref):
    rows = k_ref.shape[0]
    slot = up(rows, PAD)
    part = None
    for i, ref in enumerate((own, far)):
        x = ref[:, :LANES].astype(F32)
        x = x * x
        total = x[slot : 2 * slot]
        for h in range(1, GROUP):
            total = total + x[(1 + h) * slot : (2 + h) * slot]
        add = to_lanes(total, i) + to_lanes(x[0:slot], 2 + i)
        part = add if part is None else part + add
    x = k_ref[...].astype(F32)
    last = to_lanes(x * x, 4)
    for peer in range(out_ref.shape[0]):
        out_ref[peer, :, 0:rows] = part[:, :rows] + last
        out_ref[peer, :, rows:] = jnp.zeros((8, slot - rows), F32)


def clean_sums_body(sums_ref, out):
    out[...] = added(sums_ref)[2:4]


def listed(window_ref):
    here = lax.axis_index("seq") // 2
    found = []
    for steps in (1, 2, 3):
        at = here - steps
        hit = window_ref[here, 0] == at
        for j in range(1, window_ref.shape[1]):
            hit = hit | (window_ref[here, j] == at)
        found.append(hit & (at >= 0))
    return found


def scores(key_ref, q, rows):
    whole = rows // PAD * PAD
    s = dot(key_ref[:, :LANES], q, 1, 1)
    tail = s[whole:]
    real = lax.broadcasted_iota(jnp.int32, tail.shape, 0) < rows - whole
    return s[:whole], jnp.where(real, tail, HIDDEN)


def noisy_body(
    sums_ref, own, far, k_ref, v_ref, q_gain, k_gain,
    q_out, gt_out, keys, e_out, sum_out, stats, tall, wide,
):
    rows = k_ref.shape[0]
    slot = up(rows, PAD)
    span = GROUP * slot
    own_sum, far_sum, _, _, k_sum = to_rows(added(sums_ref)[:5])
    first = lax.axis_index("seq") % 2
    tall[...] = jnp.zeros_like(tall)
    for ref, sums, core in ((own, own_sum, first), (far, far_sum, 1 - first)):
        inv = inverse(sums, HQ)
        for h in range(GROUP):
            gain = q_gain[:, h * HEAD_SIZE : (h + 1) * HEAD_SIZE] * (SCORE_SCALE * LOG2E)
            x = ref[(1 + h) * slot : (2 + h) * slot].astype(F32)
            at = pl.ds(pl.multiple_of(core * span + h * slot, 8), slot)
            tall[at, :LANES] = x[:, :LANES] * inv * gain
            tall[at, LANES:] = x[:, LANES:]
    q_out[...] = tall[:, :LANES].astype(BF16)
    gt = tall[:, LANES:].T
    gt_out[...] = gt.astype(BF16)
    wide[rows:] = jnp.zeros((slot - rows, 2 * LANES), F32)
    wide[0:rows, :LANES] = k_ref[...].astype(F32) * inverse(k_sum, KEY_VALUE_HEADS)[:rows] * k_gain[...]
    wide[0:rows, LANES:] = v_ref[...].astype(F32)
    keys[...] = wide[...].astype(BF16)
    body, tail = scores(keys, q_out[...], rows)
    whole = body.shape[0]
    top = jnp.maximum(
        jnp.max(body, axis=0, keepdims=True), jnp.max(tail, axis=0, keepdims=True)
    )
    body = jnp.exp2(body - top)
    tail = jnp.exp2(tail - top)
    total = jnp.sum(body, axis=0, keepdims=True) + jnp.sum(tail, axis=0, keepdims=True)
    e_out[0:whole] = body.astype(BF16)
    e_out[whole:] = tail.astype(BF16)
    sums = dot(keys[:, LANES:], e_out[...], 0, 0)
    sum_out[...] = sums
    stats[...] = jnp.zeros_like(stats)
    stats[0:1] = top
    stats[1:2] = total
    stats[2:3] = jnp.sum(gt * sums, axis=0, keepdims=True)


def clean_body(
    window_ref, near, far, near_sums, far_sums, k_gain, q_ref, gt_ref, noisy_stats,
    keys, e_out, sum_out, stats, s_ref,
):
    use1, use2, use3 = listed(window_ref)
    first = lax.axis_index("seq") % 2 == 0
    from_far = jnp.logical_not(first) & use2

    def norm(ref, sums_ref):
        for j, sums in enumerate(to_rows(sums_ref[...])):
            inv = inverse(sums, KEY_VALUE_HEADS)
            raw = ref[j, :, :LANES].astype(F32)
            keys[j, :, :LANES] = (raw * inv * k_gain[...]).astype(BF16)
            keys[j, :, LANES:] = ref[j, :, LANES:]

    @pl.when(from_far)
    def _():
        norm(far, far_sums)

    @pl.when(jnp.logical_not(from_far))
    def _():
        norm(near, near_sums)

    hide = jnp.where(jnp.where(first, use1, use2 | use3), 0.0, HIDDEN)
    q = q_ref[...]
    top = None
    for j in range(2):
        body, tail = scores(keys.at[j], q, TOKENS)
        whole = body.shape[0]
        body = body + hide
        tail = tail + hide
        s_ref[j, 0:whole] = body
        s_ref[j, whole:] = tail
        here = jnp.maximum(
            jnp.max(body, axis=0, keepdims=True), jnp.max(tail, axis=0, keepdims=True)
        )
        top = here if top is None else jnp.maximum(top, here)
    total = None
    sums = None
    for j in range(2):
        e = jnp.exp2(s_ref[j] - top)
        part = jnp.sum(e, axis=0, keepdims=True)
        low = e.astype(BF16)
        e_out[j] = low
        share = dot(keys[j, :, LANES:], low, 0, 0)
        total = part if total is None else total + part
        sums = share if sums is None else sums + share
    sum_out[...] = sums
    stats[...] = noisy_stats[...]
    stats[3:4] = top
    stats[4:5] = total
    stats[5:6] = jnp.sum(gt_ref[...].astype(F32) * sums, axis=0, keepdims=True)


def key_grads(key_ref, e, gt, g, delta, q):
    dp = dot(key_ref[:, LANES:], gt, 1, 0)
    ds = (e.astype(F32) * (dp - delta)).astype(BF16)
    dv = dot(e, g, 1, 0)
    dk = dot(ds, q, 1, 0) * (1.0 / LOG2E)
    return ds, dk, dv


def clean_grad_body(
    window_ref, own, far, q_ref, gt_ref, keys, e_ref, near_out, far_out, ds_out, merged
):
    use1, use2, use3 = listed(window_ref)
    first = lax.axis_index("seq") % 2 == 0
    groups = [(ref[i : i + 1], ref[i + 1 : i + 2], ref[i + 2 : i + 3])
              for ref in (own, far) for i in (0, 3)]
    top = groups[0][0]
    for group in groups[1:]:
        top = jnp.maximum(top, group[0])
    weights = [jnp.exp2(group[0] - top) for group in groups]
    inv = 1.0 / sum(w * group[1] for w, group in zip(weights, groups))
    delta = sum(w * group[2] for w, group in zip(weights, groups)) * inv
    noisy, clean = weights[0] * inv, weights[1] * inv
    merged[...] = jnp.zeros_like(merged)
    merged[0:1] = noisy
    merged[1:2] = clean
    merged[2:3] = delta * noisy
    gt = gt_ref[...].astype(F32) * clean
    g = gt.T.astype(BF16)
    gt = gt.astype(BF16)
    q = q_ref[...]
    rows = near_out.shape[1]
    keep_near = jnp.where(jnp.where(first, use1, use3), 1.0, 0.0)
    keep_far = jnp.where(use2, 1.0, 0.0)
    for j in range(2):
        ds, dk, dv = key_grads(keys.at[j], e_ref[j], gt, g, delta * clean, q)
        ds_out[j] = ds
        for out, keep in ((near_out, keep_near), (far_out, keep_far)):
            out[j, :, :LANES] = (dk[:rows] * keep).astype(BF16)
            out[j, :, LANES:] = (dv[:rows] * keep).astype(BF16)


def noisy_grad_body(
    merged, q_ref, gt_ref, keys, clean_keys, e_ref, ds_ref, noisy_sum, clean_sum,
    grads, own, far, wide,
):
    core = lax.axis_index("seq") % 2
    span = own.shape[0] // 2
    mine = pl.ds(pl.multiple_of(core * span, 8), span)
    theirs = pl.ds(pl.multiple_of((1 - core) * span, 8), span)
    noisy = merged[0:1]
    gt = gt_ref[...].astype(F32) * noisy
    g = gt.T.astype(BF16)
    ds, dk, dv = key_grads(keys, e_ref[...], gt.astype(BF16), g, merged[2:3], q_ref[...])
    rows = grads.shape[0]
    grads[:, :LANES] = dk[:rows]
    grads[:, LANES:] = dv[:rows]
    dq = dot(keys[:, :LANES], ds, 0, 0)
    for j in range(2):
        dq = dq + dot(clean_keys[j, :, :LANES], ds_ref[j], 0, 0)
    wide[0] = (noisy_sum[...] * noisy + clean_sum[...] * merged[1:2]).T
    wide[1] = (dq * SCORE_SCALE).T
    for i in range(2):
        own[i * span : (i + 1) * span] = wide[i, mine]
        far[i * span : (i + 1) * span] = wide[i, theirs].astype(BF16)


def join_body(far, near, own_out, far_out):
    own_out[...] = near[0].astype(F32) + far[0].astype(F32)
    far_out[...] = (near[1].astype(F32) + far[1].astype(F32)).astype(BF16)


def inner_body(
    own, far, own_clean, far_clean, grads, q_ref, k_ref, c_ref, q_gain, k_gain,
    attn_out, dq_out, clean_out, grad_v, grad_cv, out_ref,
):
    clean = own_clean[...] + far_clean[...].astype(F32)
    clean_out[...] = clean
    grad_cv[...] = clean[:, LANES:].astype(BF16)
    grad_v[...] = grads[:, LANES:].astype(BF16)
    part = to_lanes(clean[:, :LANES] * k_gain[...] * c_ref[...].astype(F32), 2)
    part = part + to_lanes(grads[:, :LANES] * k_gain[...] * k_ref[...].astype(F32), 1)
    span = own.shape[0] // 2
    slot = span // GROUP
    rows = attn_out.shape[0]
    total = own[...] + far[...].astype(F32)
    for h in range(GROUP):
        cols = slice(h * HEAD_SIZE, (h + 1) * HEAD_SIZE)
        attn_out[:, cols] = total[h * slot : h * slot + rows].astype(BF16)
        at = span + h * slot
        dq_out[:, cols] = total[at : at + rows]
    part = part + to_lanes(dq_out[...] * q_gain[...] * q_ref[...].astype(F32), 0)
    for peer in range(out_ref.shape[0]):
        out_ref[peer] = part[:3]


def finish_body(
    sums_ref, inner_ref, q_ref, k_ref, c_ref, q_gain, k_gain, dq_ref, noisy_ref, clean_ref,
    grad_q, grad_k, grad_ck,
):
    rows = q_ref.shape[0]
    q_inv, _, c_inv, _, k_inv = [x[:rows] for x in to_rows(added(sums_ref)[:5])]
    q_inv = inverse(q_inv, HQ)
    k_inv = inverse(k_inv, KEY_VALUE_HEADS)
    c_inv = inverse(c_inv, KEY_VALUE_HEADS)
    q_sum, k_sum, c_sum = to_rows(added(inner_ref))
    q_pull = q_inv * q_inv * q_inv * (q_sum / (HQ * HEAD_SIZE))
    for h in range(GROUP):
        cols = slice(h * HEAD_SIZE, (h + 1) * HEAD_SIZE)
        grad_q[:, cols] = (
            q_inv * (dq_ref[:, cols] * q_gain[:, cols]) - q_ref[:, cols].astype(F32) * q_pull
        ).astype(BF16)
    width = KEY_VALUE_HEADS * HEAD_SIZE
    for inv, total, mean, ref, out in (
        (k_inv, noisy_ref, k_sum, k_ref, grad_k),
        (c_inv, clean_ref, c_sum, c_ref, grad_ck),
    ):
        pull = inv * inv * inv * (mean / width)
        out[...] = (
            inv * (total[:, :LANES] * k_gain[...]) - ref[...].astype(F32) * pull
        ).astype(BF16)


def head_exchange(value):
    return lax.all_to_all(value, "head", 0, 0)


def stretch_shift(value, steps, far):
    count = lax.axis_size("seq")
    pairs = []
    for i in range(count):
        if far and i % 2 == 0:
            continue
        length = 2 if far else (1, 3)[i % 2]
        target = i + 2 * length * steps
        if 0 <= target < count:
            pairs.append((i, target))
    return lax.ppermute(value, "seq", pairs)


def core_swap(value):
    count = lax.axis_size("seq")
    return lax.ppermute(value, "seq", [(i, i ^ 1) for i in range(count)])


def on_device(
    noisy_q, noisy_k, noisy_value, clean_k, clean_value, q_gain, key_norm_gain, out_grad, window
):
    rows = noisy_q.shape[0]
    slot = up(rows, PAD)
    span = GROUP * slot
    queries = up(2 * span, LANES)
    peers = lax.axis_size("head")
    q_gain = q_gain[None, :]
    k_gain = key_norm_gain[None, :]
    product = 2 * slot * queries * LANES
    stats = shape((8, queries), F32)
    turned = shape((LANES, queries), F32)

    fetched = (noisy_q, out_grad, clean_k, clean_value)
    packed = ((1 + GROUP) * slot, 2 * LANES)
    own = pl.pallas_call(
        pack_body,
        grid=(1,),
        out_shape=shape(packed, BF16),
        in_specs=[pl.BlockSpec(a.shape, lambda i: (0, 0)) for a in fetched],
        out_specs=pl.BlockSpec(packed, lambda i: (0, 0)),
        scratch_shapes=[pltpu.VMEM(packed, F32)],
        compiler_params=pltpu.CompilerParams(vmem_limit_bytes=58 * 2**20),
        cost_estimate=pl.CostEstimate(flops=10**10, bytes_accessed=10**6, transcendentals=0),
    )(*fetched)
    far = core_swap(own)
    pair_kv = shape((2, slot, 2 * LANES), BF16)
    clean_kv = pl.pallas_call(
        pair_body,
        grid=(1,),
        out_shape=pair_kv,
        in_specs=[pl.BlockSpec((slot, 2 * LANES), lambda i: (0, 0))] * 2,
        out_specs=pl.BlockSpec(pair_kv.shape, lambda i: (0, 0, 0)),
        compiler_params=pltpu.CompilerParams(vmem_limit_bytes=32 * 2**20),
    )(own, far)
    far_kv = stretch_shift(clean_kv, 1, True)
    near_kv = stretch_shift(clean_kv, 1, False)
    sums = kernel_call(squares_body, shape((peers, 8, slot), F32), 10**6, nargs=3)(
        own, far, noisy_k
    )
    sums = head_exchange(sums)
    clean_sums = kernel_call(clean_sums_body, shape((2, slot), F32), 10**6, nargs=1)(sums)
    far_sums = stretch_shift(clean_sums, 1, True)
    near_sums = stretch_shift(clean_sums, 1, False)
    pack = shape((slot, 2 * LANES), BF16)
    q_all, g_turned, noisy_kv, noisy_e, noisy_sum, noisy_stats = kernel_call(
        noisy_body,
        (
            shape((queries, LANES), BF16),
            shape((LANES, queries), BF16),
            pack,
            shape((slot, queries), BF16),
            turned,
            stats,
        ),
        4 * product,
        [pltpu.VMEM((queries, 2 * LANES), F32), pltpu.VMEM((slot, 2 * LANES), F32)],
        nargs=7,
    )(sums, own, far, noisy_k, noisy_value, q_gain, k_gain)
    pair = shape((2, slot, queries), BF16)
    keys, clean_e, clean_sum, own_stats = kernel_call(
        clean_body,
        (pair_kv, pair, turned, stats),
        8 * product,
        [pltpu.VMEM((2, slot, queries), F32)],
        smem=(0,),
        nargs=9,
    )(window, near_kv, far_kv, near_sums, far_sums, k_gain, q_all, g_turned, noisy_stats)
    far_stats = core_swap(own_stats)
    pair_grad = shape((2, rows, 2 * LANES), BF16)
    near_back, far_back, clean_ds, merged = kernel_call(
        clean_grad_body,
        (pair_grad, pair_grad, pair, stats),
        8 * product,
        smem=(0,),
        nargs=7,
    )(window, own_stats, far_stats, q_all, g_turned, keys, clean_e)
    far_back = stretch_shift(far_back, -1, True)
    near_back = stretch_shift(near_back, -1, False)
    noisy_grads, own, far = kernel_call(
        noisy_grad_body,
        (
            shape((rows, 2 * LANES), F32),
            shape((2 * span, LANES), F32),
            shape((2 * span, LANES), BF16),
        ),
        8 * product,
        [pltpu.VMEM((2, queries, LANES), F32)],
        nargs=9,
    )(merged, q_all, g_turned, noisy_kv, keys, noisy_e, clean_ds, noisy_sum, clean_sum)
    far = core_swap(far)
    key_grad = shape((rows, LANES), BF16)
    query_grad = shape((rows, GROUP * LANES), BF16)
    own_clean, far_clean = kernel_call(
        join_body,
        (shape((rows, 2 * LANES), F32), shape((rows, 2 * LANES), BF16)),
        10**10,
        nargs=2,
    )(far_back, near_back)
    far_clean = core_swap(far_clean)
    attn_out, dq, clean_grads, grad_v, grad_cv, inner = kernel_call(
        inner_body,
        (
            query_grad,
            shape((rows, GROUP * LANES), F32),
            shape((rows, 2 * LANES), F32),
            key_grad,
            key_grad,
            shape((peers, 3, rows), F32),
        ),
        10**6,
        nargs=10,
    )(
        own, far, own_clean, far_clean, noisy_grads, noisy_q, noisy_k, clean_k, q_gain, k_gain
    )
    inner = head_exchange(inner)
    grad_q, grad_k, grad_ck = kernel_call(
        finish_body, (query_grad, key_grad, key_grad), 10**6, nargs=10
    )(sums, inner, noisy_q, noisy_k, clean_k, q_gain, k_gain, dq, noisy_grads, clean_grads)
    return (attn_out, grad_q, grad_k, grad_v, grad_ck, grad_cv)


def solution(mesh):
    tokens = P("seq", "head")
    return jax.shard_map(
        on_device,
        mesh=mesh,
        in_specs=(tokens,) * 5 + (P("head"), P("head"), tokens, P()),
        out_specs=(tokens,) * 6,
        check_vma=False,
    )
```

```python
import math

import jax
import jax.numpy as jnp
from jax import lax
from jax.experimental import pallas as pl
from jax.experimental.pallas import tpu as pltpu
from jax.sharding import PartitionSpec as P

HEAD_SIZE = 128
KEY_VALUE_HEADS = 8
GROUP = 3
STRETCH = 520
HQ = 24
TOKENS = STRETCH // 2
EPSILON = 1e-06
HIDDEN = -1e30

PAD = 16
LANES = 128
F32 = jnp.float32
BF16 = jnp.bfloat16
SCORE_SCALE = HEAD_SIZE ** (-0.5)
LOG2E = math.log2(math.e)


def up(count, unit):
    return -(-count // unit) * unit


def shape(dims, kind):
    return jax.ShapeDtypeStruct(dims, kind)


def kernel_call(body, outs, flops, scratch=(), smem=(), nargs=0):
    specs = [pl.BlockSpec(memory_space=pltpu.SMEM if i in smem else pltpu.VMEM) for i in range(nargs)]
    size = sum(math.prod(o.shape) * o.dtype.itemsize for o in jax.tree.leaves(outs))
    return pl.pallas_call(
        body,
        out_shape=outs,
        in_specs=specs,
        out_specs=jax.tree.map(lambda o: pl.BlockSpec(memory_space=pltpu.VMEM), outs),
        scratch_shapes=list(scratch),
        compiler_params=pltpu.CompilerParams(vmem_limit_bytes=32 * 2**20),
        cost_estimate=pl.CostEstimate(flops=flops, bytes_accessed=size, transcendentals=0),
    )


def dot(a, b, ca, cb):
    return lax.dot_general(a, b, (((ca,), (cb,)), ((), ())), preferred_element_type=F32)


def halves(x):
    high = x.astype(BF16)
    return high, (x - high.astype(F32)).astype(BF16)


def to_lanes(x, row):
    pick = (lax.broadcasted_iota(jnp.int32, (8, x.shape[1]), 0) == row).astype(BF16)
    high, low = halves(x)
    return dot(pick, high, 1, 1) + dot(pick, low, 1, 1)


def to_rows(x):
    row = lax.broadcasted_iota(jnp.int32, (3, 3 * LANES), 0)
    group = lax.broadcasted_iota(jnp.int32, (3, 3 * LANES), 1) // LANES
    pick = (row == group).astype(BF16)
    high, low = halves(x)
    rows = dot(high, pick, 0, 0) + dot(low, pick, 0, 0)
    return [rows[:, i * LANES : (i + 1) * LANES] for i in range(3)]


def added(ref):
    total = ref[0]
    for i in range(1, ref.shape[0]):
        total = total + ref[i]
    return total


def inverses(ref):
    sums = to_rows(added(ref))
    widths = (HQ * HEAD_SIZE, KEY_VALUE_HEADS * HEAD_SIZE, KEY_VALUE_HEADS * HEAD_SIZE)
    return [lax.rsqrt(s / w + EPSILON) for s, w in zip(sums, widths)]


def squares_body(q_ref, k_ref, c_ref, out_ref):
    rows = None
    for i, ref in enumerate((q_ref, k_ref, c_ref)):
        x = ref[...].astype(F32)
        part = to_lanes(x * x, i)
        rows = part if rows is None else rows + part
    for peer in range(out_ref.shape[0]):
        out_ref[peer] = rows[:3]


def norms_body(
    sums_ref, q_ref, k_ref, c_ref, v_ref, cv_ref, g_ref, q_gain, k_gain, noisy_ref, out, wide, tall
):
    q_inv, k_inv, c_inv = inverses(sums_ref)
    rows = k_ref.shape[0]
    slot = up(rows, PAD)
    tall[0:rows, :LANES] = c_ref[...].astype(F32) * c_inv * k_gain[...]
    tall[0:rows, LANES:] = cv_ref[...].astype(F32)
    for h in range(GROUP):
        cols = slice(h * HEAD_SIZE, (h + 1) * HEAD_SIZE)
        gain = q_gain[:, cols] * (SCORE_SCALE * LOG2E)
        at = (1 + h) * slot
        tall[at : at + rows, :LANES] = q_ref[:, cols].astype(F32) * q_inv * gain
        tall[at : at + rows, LANES:] = g_ref[:, cols].astype(F32)
    for h in range(1 + GROUP):
        tall[h * slot + rows : (h + 1) * slot] = jnp.zeros((slot - rows, 2 * LANES), F32)
    out[...] = tall[...].astype(BF16)
    wide[rows:] = jnp.zeros((slot - rows, 2 * LANES), F32)
    wide[0:rows, 0:LANES] = k_ref[...].astype(F32) * k_inv * k_gain[...]
    wide[0:rows, LANES:] = v_ref[...].astype(F32)
    noisy_ref[...] = wide[...].astype(BF16)


def both(out, own, far):
    core = lax.axis_index("seq") % 2
    span = own.shape[0] // (1 + GROUP) * GROUP
    first = own.shape[0] - span

    @pl.when(core == 0)
    def _():
        out[0:span] = own[first:]
        out[span : 2 * span] = far[first:]

    @pl.when(core == 1)
    def _():
        out[0:span] = far[first:]
        out[span : 2 * span] = own[first:]

    out[2 * span :] = jnp.zeros((out.shape[0] - 2 * span, out.shape[1]), out.dtype)


def listed(window_ref):
    here = lax.axis_index("seq") // 2
    found = []
    for steps in (1, 2, 3):
        at = here - steps
        hit = window_ref[here, 0] == at
        for j in range(1, window_ref.shape[1]):
            hit = hit | (window_ref[here, j] == at)
        found.append(hit & (at >= 0))
    return found


def scores(key_ref, q, rows):
    whole = rows // PAD * PAD
    s = dot(key_ref[:, :LANES], q, 1, 1)
    tail = s[whole:]
    real = lax.broadcasted_iota(jnp.int32, tail.shape, 0) < rows - whole
    return s[:whole], jnp.where(real, tail, HIDDEN)


def noisy_body(own, far, keys, q_out, gt_out, e_out, sum_out, stats, rows_ref):
    both(rows_ref, own, far)
    q_out[...] = rows_ref[:, :LANES]
    gt = rows_ref[:, LANES:].astype(F32).T
    gt_out[...] = gt.astype(BF16)
    body, tail = scores(keys, q_out[...], TOKENS)
    whole = body.shape[0]
    top = jnp.maximum(
        jnp.max(body, axis=0, keepdims=True), jnp.max(tail, axis=0, keepdims=True)
    )
    body = jnp.exp2(body - top)
    tail = jnp.exp2(tail - top)
    total = jnp.sum(body, axis=0, keepdims=True) + jnp.sum(tail, axis=0, keepdims=True)
    e_out[0:whole] = body.astype(BF16)
    e_out[whole:] = tail.astype(BF16)
    sums = dot(keys[:, LANES:], e_out[...], 0, 0)
    sum_out[...] = sums
    stats[...] = jnp.zeros_like(stats)
    stats[0:1] = top
    stats[1:2] = total
    stats[2:3] = jnp.sum(gt * sums, axis=0, keepdims=True)


def pair_body(own, far, out):
    slot = out.shape[1]
    out[0] = own[0:slot]
    out[1] = far[0:slot]


def clean_body(
    window_ref, near, far, q_ref, gt_ref, noisy_stats, keys, e_out, sum_out, stats, s_ref
):
    use1, use2, use3 = listed(window_ref)
    first = lax.axis_index("seq") % 2 == 0
    from_far = jnp.logical_not(first) & use2

    @pl.when(from_far)
    def _():
        keys[...] = far[...]

    @pl.when(jnp.logical_not(from_far))
    def _():
        keys[...] = near[...]

    hide = jnp.where(jnp.where(first, use1, use2 | use3), 0.0, HIDDEN)
    q = q_ref[...]
    top = None
    for j in range(2):
        body, tail = scores(keys.at[j], q, TOKENS)
        whole = body.shape[0]
        body = body + hide
        tail = tail + hide
        s_ref[j, 0:whole] = body
        s_ref[j, whole:] = tail
        here = jnp.maximum(
            jnp.max(body, axis=0, keepdims=True), jnp.max(tail, axis=0, keepdims=True)
        )
        top = here if top is None else jnp.maximum(top, here)
    total = None
    sums = None
    for j in range(2):
        e = jnp.exp2(s_ref[j] - top)
        part = jnp.sum(e, axis=0, keepdims=True)
        low = e.astype(BF16)
        e_out[j] = low
        share = dot(keys[j, :, LANES:], low, 0, 0)
        total = part if total is None else total + part
        sums = share if sums is None else sums + share
    sum_out[...] = sums
    stats[...] = noisy_stats[...]
    stats[3:4] = top
    stats[4:5] = total
    stats[5:6] = jnp.sum(gt_ref[...].astype(F32) * sums, axis=0, keepdims=True)


def key_grads(key_ref, e, gt, g, delta, q):
    dp = dot(key_ref[:, LANES:], gt, 1, 0)
    ds = (e.astype(F32) * (dp - delta)).astype(BF16)
    dv = dot(e, g, 1, 0)
    dk = dot(ds, q, 1, 0) * (1.0 / LOG2E)
    return ds, dk, dv


def clean_grad_body(
    window_ref, own, far, q_ref, gt_ref, keys, e_ref, near_out, far_out, ds_out, merged
):
    use1, use2, use3 = listed(window_ref)
    first = lax.axis_index("seq") % 2 == 0
    groups = [(ref[i : i + 1], ref[i + 1 : i + 2], ref[i + 2 : i + 3])
              for ref in (own, far) for i in (0, 3)]
    top = groups[0][0]
    for group in groups[1:]:
        top = jnp.maximum(top, group[0])
    weights = [jnp.exp2(group[0] - top) for group in groups]
    inv = 1.0 / sum(w * group[1] for w, group in zip(weights, groups))
    delta = sum(w * group[2] for w, group in zip(weights, groups)) * inv
    noisy, clean = weights[0] * inv, weights[1] * inv
    merged[...] = jnp.zeros_like(merged)
    merged[0:1] = noisy
    merged[1:2] = clean
    merged[2:3] = delta * noisy
    gt = gt_ref[...].astype(F32) * clean
    g = gt.T.astype(BF16)
    gt = gt.astype(BF16)
    q = q_ref[...]
    rows = near_out.shape[1]
    keep_near = jnp.where(jnp.where(first, use1, use3), 1.0, 0.0)
    keep_far = jnp.where(use2, 1.0, 0.0)
    for j in range(2):
        ds, dk, dv = key_grads(keys.at[j], e_ref[j], gt, g, delta * clean, q)
        ds_out[j] = ds
        for out, keep in ((near_out, keep_near), (far_out, keep_far)):
            out[j, :, :LANES] = (dk[:rows] * keep).astype(BF16)
            out[j, :, LANES:] = (dv[:rows] * keep).astype(BF16)


def noisy_grad_body(
    merged, q_ref, gt_ref, keys, clean_keys, e_ref, ds_ref, noisy_sum, clean_sum,
    grads, own, far, wide,
):
    core = lax.axis_index("seq") % 2
    span = own.shape[0] // 2
    mine = pl.ds(pl.multiple_of(core * span, 8), span)
    theirs = pl.ds(pl.multiple_of((1 - core) * span, 8), span)
    noisy = merged[0:1]
    gt = gt_ref[...].astype(F32) * noisy
    g = gt.T.astype(BF16)
    ds, dk, dv = key_grads(keys, e_ref[...], gt.astype(BF16), g, merged[2:3], q_ref[...])
    rows = grads.shape[0]
    grads[:, :LANES] = dk[:rows]
    grads[:, LANES:] = dv[:rows]
    dq = dot(keys[:, :LANES], ds, 0, 0)
    for j in range(2):
        dq = dq + dot(clean_keys[j, :, :LANES], ds_ref[j], 0, 0)
    wide[0] = (noisy_sum[...] * noisy + clean_sum[...] * merged[1:2]).T
    wide[1] = (dq * SCORE_SCALE).T
    for i in range(2):
        own[i * span : (i + 1) * span] = wide[i, mine]
        far[i * span : (i + 1) * span] = wide[i, theirs].astype(BF16)


def join_body(far, near, own_out, far_out):
    own_out[...] = near[0].astype(F32) + far[0].astype(F32)
    far_out[...] = (near[1].astype(F32) + far[1].astype(F32)).astype(BF16)


def settle_body(own, far, grads, q_ref, k_ref, q_gain, k_gain, attn_out, dq_out, grad_v, sums):
    grad_v[...] = grads[:, LANES:].astype(BF16)
    part = to_lanes(grads[:, :LANES] * k_gain[...] * k_ref[...].astype(F32), 1)
    span = own.shape[0] // 2
    slot = span // GROUP
    rows = attn_out.shape[0]
    total = own[...] + far[...].astype(F32)
    for h in range(GROUP):
        cols = slice(h * HEAD_SIZE, (h + 1) * HEAD_SIZE)
        attn_out[:, cols] = total[h * slot : h * slot + rows].astype(BF16)
        at = span + h * slot
        dq_out[:, cols] = total[at : at + rows]
    sums[...] = part + to_lanes(dq_out[...] * q_gain[...] * q_ref[...].astype(F32), 0)


def inner_body(own_clean, far_clean, c_ref, k_gain, sums, clean_out, grad_cv, out_ref):
    clean = own_clean[...] + far_clean[...].astype(F32)
    clean_out[...] = clean
    grad_cv[...] = clean[:, LANES:].astype(BF16)
    part = sums[...] + to_lanes(clean[:, :LANES] * k_gain[...] * c_ref[...].astype(F32), 2)
    for peer in range(out_ref.shape[0]):
        out_ref[peer] = part[:3]


def finish_body(
    sums_ref, inner_ref, q_ref, k_ref, c_ref, q_gain, k_gain, dq_ref, noisy_ref, clean_ref,
    grad_q, grad_k, grad_ck,
):
    q_inv, k_inv, c_inv = inverses(sums_ref)
    q_sum, k_sum, c_sum = to_rows(added(inner_ref))
    q_pull = q_inv * q_inv * q_inv * (q_sum / (HQ * HEAD_SIZE))
    for h in range(GROUP):
        cols = slice(h * HEAD_SIZE, (h + 1) * HEAD_SIZE)
        grad_q[:, cols] = (
            q_inv * (dq_ref[:, cols] * q_gain[:, cols]) - q_ref[:, cols].astype(F32) * q_pull
        ).astype(BF16)
    width = KEY_VALUE_HEADS * HEAD_SIZE
    for inv, total, mean, ref, out in (
        (k_inv, noisy_ref, k_sum, k_ref, grad_k),
        (c_inv, clean_ref, c_sum, c_ref, grad_ck),
    ):
        pull = inv * inv * inv * (mean / width)
        out[...] = (
            inv * (total[:, :LANES] * k_gain[...]) - ref[...].astype(F32) * pull
        ).astype(BF16)


def head_exchange(value):
    return lax.all_to_all(value, "head", 0, 0)


def stretch_shift(value, steps, far):
    count = lax.axis_size("seq")
    pairs = []
    for i in range(count):
        if far and i % 2 == 0:
            continue
        length = 2 if far else (1, 3)[i % 2]
        target = i + 2 * length * steps
        if 0 <= target < count:
            pairs.append((i, target))
    return lax.ppermute(value, "seq", pairs)


def core_swap(value):
    count = lax.axis_size("seq")
    return lax.ppermute(value, "seq", [(i, i ^ 1) for i in range(count)])


def on_device(
    noisy_q, noisy_k, noisy_value, clean_k, clean_value, q_gain, key_norm_gain, out_grad, window
):
    rows = noisy_q.shape[0]
    slot = up(rows, PAD)
    span = GROUP * slot
    queries = up(2 * span, LANES)
    peers = lax.axis_size("head")
    q_gain = q_gain[None, :]
    k_gain = key_norm_gain[None, :]
    product = 2 * slot * queries * LANES
    stats = shape((8, queries), F32)
    turned = shape((LANES, queries), F32)

    fetched = (noisy_q, noisy_k, clean_k)
    sums = pl.pallas_call(
        squares_body,
        grid=(1,),
        out_shape=shape((peers, 3, rows), F32),
        in_specs=[pl.BlockSpec(a.shape, lambda i: (0, 0)) for a in fetched],
        out_specs=pl.BlockSpec((peers, 3, rows), lambda i: (0, 0, 0)),
        compiler_params=pltpu.CompilerParams(vmem_limit_bytes=60 * 2**20),
        cost_estimate=pl.CostEstimate(flops=10**10, bytes_accessed=10**6, transcendentals=0),
    )(*fetched)
    sums = head_exchange(sums)
    pack = shape((slot, 2 * LANES), BF16)
    packed = ((1 + GROUP) * slot, 2 * LANES)
    noisy_kv, own = kernel_call(
        norms_body,
        (pack, shape(packed, BF16)),
        10**6,
        [pltpu.VMEM((slot, 2 * LANES), F32), pltpu.VMEM(packed, F32)],
        nargs=9,
    )(sums, noisy_q, noisy_k, clean_k, noisy_value, clean_value, out_grad, q_gain, k_gain)
    far = core_swap(own)
    pair_kv = shape((2, slot, 2 * LANES), BF16)
    clean_kv = kernel_call(pair_body, pair_kv, 10**6, nargs=2)(own, far)
    near_kv = stretch_shift(clean_kv, 1, False)
    far_kv = stretch_shift(clean_kv, 1, True)
    q_all, g_turned, noisy_e, noisy_sum, noisy_stats = kernel_call(
        noisy_body,
        (
            shape((queries, LANES), BF16),
            shape((LANES, queries), BF16),
            shape((slot, queries), BF16),
            turned,
            stats,
        ),
        4 * product,
        [pltpu.VMEM((queries, 2 * LANES), BF16)],
        nargs=3,
    )(own, far, noisy_kv)
    pair = shape((2, slot, queries), BF16)
    keys, clean_e, clean_sum, own_stats = kernel_call(
        clean_body,
        (pair_kv, pair, turned, stats),
        8 * product,
        [pltpu.VMEM((2, slot, queries), F32)],
        smem=(0,),
        nargs=6,
    )(window, near_kv, far_kv, q_all, g_turned, noisy_stats)
    far_stats = core_swap(own_stats)
    pair_grad = shape((2, rows, 2 * LANES), BF16)
    near_back, far_back, clean_ds, merged = kernel_call(
        clean_grad_body,
        (pair_grad, pair_grad, pair, stats),
        8 * product,
        smem=(0,),
        nargs=7,
    )(window, own_stats, far_stats, q_all, g_turned, keys, clean_e)
    far_back = stretch_shift(far_back, -1, True)
    near_back = stretch_shift(near_back, -1, False)
    noisy_grads, own, far = kernel_call(
        noisy_grad_body,
        (
            shape((rows, 2 * LANES), F32),
            shape((2 * span, LANES), F32),
            shape((2 * span, LANES), BF16),
        ),
        8 * product,
        [pltpu.VMEM((2, queries, LANES), F32)],
        nargs=9,
    )(merged, q_all, g_turned, noisy_kv, keys, noisy_e, clean_ds, noisy_sum, clean_sum)
    far = core_swap(far)
    key_grad = shape((rows, LANES), BF16)
    query_grad = shape((rows, GROUP * LANES), BF16)
    own_clean, far_clean = kernel_call(
        join_body,
        (shape((rows, 2 * LANES), F32), shape((rows, 2 * LANES), BF16)),
        10**10,
        nargs=2,
    )(far_back, near_back)
    far_clean = core_swap(far_clean)
    attn_out, dq, grad_v, inner = kernel_call(
        settle_body,
        (query_grad, shape((rows, GROUP * LANES), F32), key_grad, shape((8, rows), F32)),
        10**6,
        nargs=7,
    )(own, far, noisy_grads, noisy_q, noisy_k, q_gain, k_gain)
    clean_grads, grad_cv, inner = kernel_call(
        inner_body,
        (shape((rows, 2 * LANES), F32), key_grad, shape((peers, 3, rows), F32)),
        10**6,
        nargs=5,
    )(own_clean, far_clean, clean_k, k_gain, inner)
    inner = head_exchange(inner)
    grad_q, grad_k, grad_ck = kernel_call(
        finish_body, (query_grad, key_grad, key_grad), 10**6, nargs=10
    )(sums, inner, noisy_q, noisy_k, clean_k, q_gain, k_gain, dq, noisy_grads, clean_grads)
    return (attn_out, grad_q, grad_k, grad_v, grad_ck, grad_cv)


def solution(mesh):
    tokens = P("seq", "head")
    return jax.shard_map(
        on_device,
        mesh=mesh,
        in_specs=(tokens,) * 5 + (P("head"), P("head"), tokens, P()),
        out_specs=(tokens,) * 6,
        check_vma=False,
    )
```

```python
import math

import jax
import jax.numpy as jnp
from jax import lax
from jax.experimental import pallas as pl
from jax.experimental.pallas import tpu as pltpu
from jax.sharding import PartitionSpec as P

HEAD_SIZE = 128
KEY_VALUE_HEADS = 8
GROUP = 3
STRETCH = 520
HQ = 24
TOKENS = STRETCH // 2
EPSILON = 1e-06
HIDDEN = -1e30

PAD = 16
LANES = 128
F32 = jnp.float32
BF16 = jnp.bfloat16
SCORE_SCALE = HEAD_SIZE ** (-0.5)
LOG2E = math.log2(math.e)


def up(count, unit):
    return -(-count // unit) * unit


def shape(dims, kind):
    return jax.ShapeDtypeStruct(dims, kind)


def kernel_call(body, outs, flops, scratch=(), smem=(), nargs=0):
    specs = [pl.BlockSpec(memory_space=pltpu.SMEM if i in smem else pltpu.VMEM) for i in range(nargs)]
    size = sum(math.prod(o.shape) * o.dtype.itemsize for o in jax.tree.leaves(outs))
    return pl.pallas_call(
        body,
        out_shape=outs,
        in_specs=specs,
        out_specs=jax.tree.map(lambda o: pl.BlockSpec(memory_space=pltpu.VMEM), outs),
        scratch_shapes=list(scratch),
        compiler_params=pltpu.CompilerParams(vmem_limit_bytes=32 * 2**20),
        cost_estimate=pl.CostEstimate(flops=flops, bytes_accessed=size, transcendentals=0),
    )


def dot(a, b, ca, cb):
    return lax.dot_general(a, b, (((ca,), (cb,)), ((), ())), preferred_element_type=F32)


def halves(x):
    high = x.astype(BF16)
    return high, (x - high.astype(F32)).astype(BF16)


def to_lanes(x, row):
    pick = (lax.broadcasted_iota(jnp.int32, (8, x.shape[1]), 0) == row).astype(BF16)
    high, low = halves(x)
    return dot(pick, high, 1, 1) + dot(pick, low, 1, 1)


def to_rows(x):
    row = lax.broadcasted_iota(jnp.int32, (3, 3 * LANES), 0)
    group = lax.broadcasted_iota(jnp.int32, (3, 3 * LANES), 1) // LANES
    pick = (row == group).astype(BF16)
    high, low = halves(x)
    rows = dot(high, pick, 0, 0) + dot(low, pick, 0, 0)
    return [rows[:, i * LANES : (i + 1) * LANES] for i in range(3)]


def added(ref):
    total = ref[0]
    for i in range(1, ref.shape[0]):
        total = total + ref[i]
    return total


def inverses(ref):
    sums = to_rows(added(ref))
    widths = (HQ * HEAD_SIZE, KEY_VALUE_HEADS * HEAD_SIZE, KEY_VALUE_HEADS * HEAD_SIZE)
    return [lax.rsqrt(s / w + EPSILON) for s, w in zip(sums, widths)]


def squares_body(q_ref, k_ref, c_ref, out_ref):
    rows = None
    for i, ref in enumerate((q_ref, k_ref, c_ref)):
        x = ref[...].astype(F32)
        part = to_lanes(x * x, i)
        rows = part if rows is None else rows + part
    for peer in range(out_ref.shape[0]):
        out_ref[peer] = rows[:3]


def norms_body(
    sums_ref, q_ref, k_ref, c_ref, v_ref, cv_ref, g_ref, q_gain, k_gain, noisy_ref, out, wide, tall
):
    q_inv, k_inv, c_inv = inverses(sums_ref)
    rows = k_ref.shape[0]
    slot = up(rows, PAD)
    tall[0:rows, :LANES] = c_ref[...].astype(F32) * c_inv * k_gain[...]
    tall[0:rows, LANES:] = cv_ref[...].astype(F32)
    for h in range(GROUP):
        cols = slice(h * HEAD_SIZE, (h + 1) * HEAD_SIZE)
        gain = q_gain[:, cols] * (SCORE_SCALE * LOG2E)
        at = (1 + h) * slot
        tall[at : at + rows, :LANES] = q_ref[:, cols].astype(F32) * q_inv * gain
        tall[at : at + rows, LANES:] = g_ref[:, cols].astype(F32)
    for h in range(1 + GROUP):
        tall[h * slot + rows : (h + 1) * slot] = jnp.zeros((slot - rows, 2 * LANES), F32)
    out[...] = tall[...].astype(BF16)
    wide[rows:] = jnp.zeros((slot - rows, 2 * LANES), F32)
    wide[0:rows, 0:LANES] = k_ref[...].astype(F32) * k_inv * k_gain[...]
    wide[0:rows, LANES:] = v_ref[...].astype(F32)
    noisy_ref[...] = wide[...].astype(BF16)


def both(out, own, far):
    core = lax.axis_index("seq") % 2
    span = own.shape[0] // (1 + GROUP) * GROUP
    first = own.shape[0] - span

    @pl.when(core == 0)
    def _():
        out[0:span] = own[first:]
        out[span : 2 * span] = far[first:]

    @pl.when(core == 1)
    def _():
        out[0:span] = far[first:]
        out[span : 2 * span] = own[first:]

    out[2 * span :] = jnp.zeros((out.shape[0] - 2 * span, out.shape[1]), out.dtype)


def listed(window_ref):
    here = lax.axis_index("seq") // 2
    found = []
    for steps in (1, 2, 3):
        at = here - steps
        hit = window_ref[here, 0] == at
        for j in range(1, window_ref.shape[1]):
            hit = hit | (window_ref[here, j] == at)
        found.append(hit & (at >= 0))
    return found


def scores(key_ref, q, rows):
    whole = rows // PAD * PAD
    s = dot(key_ref[:, :LANES], q, 1, 1)
    tail = s[whole:]
    real = lax.broadcasted_iota(jnp.int32, tail.shape, 0) < rows - whole
    return s[:whole], jnp.where(real, tail, HIDDEN)


def noisy_body(own, far, keys, q_out, gt_out, e_out, sum_out, stats, rows_ref):
    both(rows_ref, own, far)
    q_out[...] = rows_ref[:, :LANES]
    gt = rows_ref[:, LANES:].astype(F32).T
    gt_out[...] = gt.astype(BF16)
    body, tail = scores(keys, q_out[...], TOKENS)
    whole = body.shape[0]
    top = jnp.maximum(
        jnp.max(body, axis=0, keepdims=True), jnp.max(tail, axis=0, keepdims=True)
    )
    body = jnp.exp2(body - top)
    tail = jnp.exp2(tail - top)
    total = jnp.sum(body, axis=0, keepdims=True) + jnp.sum(tail, axis=0, keepdims=True)
    e_out[0:whole] = body.astype(BF16)
    e_out[whole:] = tail.astype(BF16)
    sums = dot(keys[:, LANES:], e_out[...], 0, 0)
    sum_out[...] = sums
    stats[...] = jnp.zeros_like(stats)
    stats[0:1] = top
    stats[1:2] = total
    stats[2:3] = jnp.sum(gt * sums, axis=0, keepdims=True)


def pair_body(own, far, out):
    slot = out.shape[1]
    out[0] = own[0:slot]
    out[1] = far[0:slot]


def clean_body(
    window_ref, near, far, q_ref, gt_ref, noisy_stats, keys, e_out, sum_out, stats, s_ref
):
    use1, use2, use3 = listed(window_ref)
    first = lax.axis_index("seq") % 2 == 0
    from_far = jnp.logical_not(first) & use2

    @pl.when(from_far)
    def _():
        keys[...] = far[...]

    @pl.when(jnp.logical_not(from_far))
    def _():
        keys[...] = near[...]

    hide = jnp.where(jnp.where(first, use1, use2 | use3), 0.0, HIDDEN)
    q = q_ref[...]
    top = None
    for j in range(2):
        body, tail = scores(keys.at[j], q, TOKENS)
        whole = body.shape[0]
        body = body + hide
        tail = tail + hide
        s_ref[j, 0:whole] = body
        s_ref[j, whole:] = tail
        here = jnp.maximum(
            jnp.max(body, axis=0, keepdims=True), jnp.max(tail, axis=0, keepdims=True)
        )
        top = here if top is None else jnp.maximum(top, here)
    total = None
    sums = None
    for j in range(2):
        e = jnp.exp2(s_ref[j] - top)
        part = jnp.sum(e, axis=0, keepdims=True)
        low = e.astype(BF16)
        e_out[j] = low
        share = dot(keys[j, :, LANES:], low, 0, 0)
        total = part if total is None else total + part
        sums = share if sums is None else sums + share
    sum_out[...] = sums
    stats[...] = noisy_stats[...]
    stats[3:4] = top
    stats[4:5] = total
    stats[5:6] = jnp.sum(gt_ref[...].astype(F32) * sums, axis=0, keepdims=True)


def products_body(keys, gt_ref, out):
    for j in range(2):
        out[j] = dot(keys[j, :, LANES:], gt_ref[...], 1, 0)


def clean_grad_body(
    window_ref, own, far, q_ref, gt_ref, dp_ref, e_ref, near_out, far_out, ds_out, merged
):
    use1, use2, use3 = listed(window_ref)
    first = lax.axis_index("seq") % 2 == 0
    groups = [(ref[i : i + 1], ref[i + 1 : i + 2], ref[i + 2 : i + 3])
              for ref in (own, far) for i in (0, 3)]
    top = groups[0][0]
    for group in groups[1:]:
        top = jnp.maximum(top, group[0])
    weights = [jnp.exp2(group[0] - top) for group in groups]
    inv = 1.0 / sum(w * group[1] for w, group in zip(weights, groups))
    delta = sum(w * group[2] for w, group in zip(weights, groups)) * inv
    noisy, clean = weights[0] * inv, weights[1] * inv
    merged[...] = jnp.zeros_like(merged)
    merged[0:1] = noisy
    merged[1:2] = clean
    merged[2:3] = delta * noisy
    gt = (gt_ref[...].astype(F32) * clean).astype(BF16)
    delta = delta * clean
    q = q_ref[...]
    rows = near_out.shape[1]
    keep_near = jnp.where(jnp.where(first, use1, use3), 1.0, 0.0)
    keep_far = jnp.where(use2, 1.0, 0.0)
    for j in range(2):
        e = e_ref[j]
        ds = (e.astype(F32) * (dp_ref[j] * clean - delta)).astype(BF16)
        ds_out[j] = ds
        dk = dot(ds, q, 1, 0) * (1.0 / LOG2E)
        dv = dot(e, gt, 1, 1)
        for out, keep in ((near_out, keep_near), (far_out, keep_far)):
            out[j, :, :LANES] = (dk[:rows] * keep).astype(BF16)
            out[j, :, LANES:] = (dv[:rows] * keep).astype(BF16)


def noisy_grad_body(
    merged, q_ref, gt_ref, keys, clean_keys, e_ref, ds_ref, noisy_sum, clean_sum,
    grads, own, far, wide,
):
    core = lax.axis_index("seq") % 2
    span = own.shape[0] // 2
    mine = pl.ds(pl.multiple_of(core * span, 8), span)
    theirs = pl.ds(pl.multiple_of((1 - core) * span, 8), span)
    noisy = merged[0:1]
    gt = (gt_ref[...].astype(F32) * noisy).astype(BF16)
    e = e_ref[...]
    dp = dot(keys[:, LANES:], gt, 1, 0)
    ds = (e.astype(F32) * (dp - merged[2:3])).astype(BF16)
    dk = dot(ds, q_ref[...], 1, 0) * (1.0 / LOG2E)
    dv = dot(e, gt, 1, 1)
    rows = grads.shape[0]
    grads[:, :LANES] = dk[:rows]
    grads[:, LANES:] = dv[:rows]
    dq = dot(keys[:, :LANES], ds, 0, 0)
    for j in range(2):
        dq = dq + dot(clean_keys[j, :, :LANES], ds_ref[j], 0, 0)
    wide[0] = (noisy_sum[...] * noisy + clean_sum[...] * merged[1:2]).T
    wide[1] = (dq * SCORE_SCALE).T
    for i in range(2):
        own[i * span : (i + 1) * span] = wide[i, mine]
        far[i * span : (i + 1) * span] = wide[i, theirs].astype(BF16)


def join_body(far, near, own_out, far_out):
    own_out[...] = near[0].astype(F32) + far[0].astype(F32)
    far_out[...] = (near[1].astype(F32) + far[1].astype(F32)).astype(BF16)


def settle_body(
    sums_ref, own, far, grads, q_ref, k_ref, c_ref, q_gain, k_gain,
    attn_out, grad_v, sums, q_push, q_pull, k_push, k_pull, c_scale, c_pull,
):
    q_inv, k_inv, c_inv = inverses(sums_ref)
    grad_v[...] = grads[:, LANES:].astype(BF16)
    span = own.shape[0] // 2
    slot = span // GROUP
    rows = attn_out.shape[0]
    total = own[...] + far[...].astype(F32)
    cube = q_inv * q_inv * q_inv * (1.0 / (HQ * HEAD_SIZE))
    inner = None
    for h in range(GROUP):
        cols = slice(h * HEAD_SIZE, (h + 1) * HEAD_SIZE)
        attn_out[:, cols] = total[h * slot : h * slot + rows].astype(BF16)
        at = span + h * slot
        scaled = total[at : at + rows] * q_gain[:, cols]
        x = q_ref[:, cols].astype(F32)
        q_push[:, cols] = scaled * q_inv
        q_pull[:, cols] = x * cube
        inner = scaled * x if inner is None else inner + scaled * x
    width = 1.0 / (KEY_VALUE_HEADS * HEAD_SIZE)
    x = k_ref[...].astype(F32)
    scaled = grads[:, :LANES] * k_gain[...]
    k_push[...] = scaled * k_inv
    k_pull[...] = x * (k_inv * k_inv * k_inv * width)
    c_scale[...] = c_inv
    c_pull[...] = c_ref[...].astype(F32) * (c_inv * c_inv * c_inv * width)
    sums[...] = to_lanes(inner, 0) + to_lanes(scaled * x, 1)


def inner_body(own_clean, far_clean, c_ref, k_gain, c_scale, sums, c_push, grad_cv, out_ref):
    clean = own_clean[...] + far_clean[...].astype(F32)
    grad_cv[...] = clean[:, LANES:].astype(BF16)
    scaled = clean[:, :LANES] * k_gain[...]
    c_push[...] = scaled * c_scale[...]
    part = sums[...] + to_lanes(scaled * c_ref[...].astype(F32), 2)
    for peer in range(out_ref.shape[0]):
        out_ref[peer] = part[:3]


def finish_body(
    inner_ref, q_push, q_pull, k_push, k_pull, c_push, c_pull, grad_q, grad_k, grad_ck
):
    q_sum, k_sum, c_sum = to_rows(added(inner_ref))
    for h in range(GROUP):
        cols = slice(h * HEAD_SIZE, (h + 1) * HEAD_SIZE)
        grad_q[:, cols] = (q_push[:, cols] - q_pull[:, cols] * q_sum).astype(BF16)
    grad_k[...] = (k_push[...] - k_pull[...] * k_sum).astype(BF16)
    grad_ck[...] = (c_push[...] - c_pull[...] * c_sum).astype(BF16)


def head_exchange(value):
    return lax.all_to_all(value, "head", 0, 0)


def stretch_shift(value, steps, far):
    count = lax.axis_size("seq")
    pairs = []
    for i in range(count):
        if far and i % 2 == 0:
            continue
        length = 2 if far else (1, 3)[i % 2]
        target = i + 2 * length * steps
        if 0 <= target < count:
            pairs.append((i, target))
    return lax.ppermute(value, "seq", pairs)


def core_swap(value):
    count = lax.axis_size("seq")
    return lax.ppermute(value, "seq", [(i, i ^ 1) for i in range(count)])


def on_device(
    noisy_q, noisy_k, noisy_value, clean_k, clean_value, q_gain, key_norm_gain, out_grad, window
):
    rows = noisy_q.shape[0]
    slot = up(rows, PAD)
    span = GROUP * slot
    queries = up(2 * span, LANES)
    peers = lax.axis_size("head")
    q_gain = q_gain[None, :]
    k_gain = key_norm_gain[None, :]
    product = 2 * slot * queries * LANES
    stats = shape((8, queries), F32)
    turned = shape((LANES, queries), F32)

    fetched = (noisy_q, noisy_k, clean_k)
    sums = pl.pallas_call(
        squares_body,
        grid=(1,),
        out_shape=shape((peers, 3, rows), F32),
        in_specs=[pl.BlockSpec(a.shape, lambda i: (0, 0)) for a in fetched],
        out_specs=pl.BlockSpec((peers, 3, rows), lambda i: (0, 0, 0)),
        compiler_params=pltpu.CompilerParams(vmem_limit_bytes=60 * 2**20),
        cost_estimate=pl.CostEstimate(flops=10**10, bytes_accessed=10**6, transcendentals=0),
    )(*fetched)
    sums = head_exchange(sums)
    pack = shape((slot, 2 * LANES), BF16)
    packed = ((1 + GROUP) * slot, 2 * LANES)
    noisy_kv, own = kernel_call(
        norms_body,
        (pack, shape(packed, BF16)),
        10**6,
        [pltpu.VMEM((slot, 2 * LANES), F32), pltpu.VMEM(packed, F32)],
        nargs=9,
    )(sums, noisy_q, noisy_k, clean_k, noisy_value, clean_value, out_grad, q_gain, k_gain)
    far = core_swap(own)
    pair_kv = shape((2, slot, 2 * LANES), BF16)
    clean_kv = kernel_call(pair_body, pair_kv, 10**6, nargs=2)(own, far)
    near_kv = stretch_shift(clean_kv, 1, False)
    far_kv = stretch_shift(clean_kv, 1, True)
    q_all, g_turned, noisy_e, noisy_sum, noisy_stats = kernel_call(
        noisy_body,
        (
            shape((queries, LANES), BF16),
            shape((LANES, queries), BF16),
            shape((slot, queries), BF16),
            turned,
            stats,
        ),
        4 * product,
        [pltpu.VMEM((queries, 2 * LANES), BF16)],
        nargs=3,
    )(own, far, noisy_kv)
    pair = shape((2, slot, queries), BF16)
    keys, clean_e, clean_sum, own_stats = kernel_call(
        clean_body,
        (pair_kv, pair, turned, stats),
        8 * product,
        [pltpu.VMEM((2, slot, queries), F32)],
        smem=(0,),
        nargs=6,
    )(window, near_kv, far_kv, q_all, g_turned, noisy_stats)
    far_stats = core_swap(own_stats)
    products = kernel_call(
        products_body, shape((2, slot, queries), F32), 2 * product, nargs=2
    )(keys, g_turned)
    pair_grad = shape((2, rows, 2 * LANES), BF16)
    near_back, far_back, clean_ds, merged = kernel_call(
        clean_grad_body,
        (pair_grad, pair_grad, pair, stats),
        8 * product,
        smem=(0,),
        nargs=7,
    )(window, own_stats, far_stats, q_all, g_turned, products, clean_e)
    far_back = stretch_shift(far_back, -1, True)
    near_back = stretch_shift(near_back, -1, False)
    noisy_grads, own, far = kernel_call(
        noisy_grad_body,
        (
            shape((rows, 2 * LANES), F32),
            shape((2 * span, LANES), F32),
            shape((2 * span, LANES), BF16),
        ),
        8 * product,
        [pltpu.VMEM((2, queries, LANES), F32)],
        nargs=9,
    )(merged, q_all, g_turned, noisy_kv, keys, noisy_e, clean_ds, noisy_sum, clean_sum)
    far = core_swap(far)
    key_grad = shape((rows, LANES), BF16)
    query_grad = shape((rows, GROUP * LANES), BF16)
    own_clean, far_clean = kernel_call(
        join_body,
        (shape((rows, 2 * LANES), F32), shape((rows, 2 * LANES), BF16)),
        10**10,
        nargs=2,
    )(far_back, near_back)
    far_clean = core_swap(far_clean)
    query_wide = shape((rows, GROUP * LANES), F32)
    key_wide = shape((rows, LANES), F32)
    attn_out, grad_v, inner, q_push, q_pull, k_push, k_pull, c_scale, c_pull = kernel_call(
        settle_body,
        (query_grad, key_grad, shape((8, rows), F32), query_wide, query_wide)
        + (key_wide,) * 4,
        10**6,
        nargs=9,
    )(sums, own, far, noisy_grads, noisy_q, noisy_k, clean_k, q_gain, k_gain)
    c_push, grad_cv, inner = kernel_call(
        inner_body,
        (key_wide, key_grad, shape((peers, 3, rows), F32)),
        10**6,
        nargs=6,
    )(own_clean, far_clean, clean_k, k_gain, c_scale, inner)
    inner = head_exchange(inner)
    grad_q, grad_k, grad_ck = kernel_call(
        finish_body, (query_grad, key_grad, key_grad), 10**6, nargs=7
    )(inner, q_push, q_pull, k_push, k_pull, c_push, c_pull)
    return (attn_out, grad_q, grad_k, grad_v, grad_ck, grad_cv)


def solution(mesh):
    tokens = P("seq", "head")
    return jax.shard_map(
        on_device,
        mesh=mesh,
        in_specs=(tokens,) * 5 + (P("head"), P("head"), tokens, P()),
        out_specs=(tokens,) * 6,
        check_vma=False,
    )
```

```python
import math

import jax
import jax.numpy as jnp
from jax import lax
from jax.experimental import pallas as pl
from jax.experimental.pallas import tpu as pltpu
from jax.sharding import PartitionSpec as P

HEAD_SIZE = 128
KEY_VALUE_HEADS = 8
GROUP = 3
STRETCH = 520
HQ = 24
TOKENS = STRETCH // 2
EPSILON = 1e-06
HIDDEN = -1e30

PAD = 16
LANES = 128
F32 = jnp.float32
BF16 = jnp.bfloat16
SCORE_SCALE = HEAD_SIZE ** (-0.5)
LOG2E = math.log2(math.e)


def up(count, unit):
    return -(-count // unit) * unit


def shape(dims, kind):
    return jax.ShapeDtypeStruct(dims, kind)


def kernel_call(body, outs, flops, scratch=(), smem=(), nargs=0):
    specs = [pl.BlockSpec(memory_space=pltpu.SMEM if i in smem else pltpu.VMEM) for i in range(nargs)]
    size = sum(math.prod(o.shape) * o.dtype.itemsize for o in jax.tree.leaves(outs))
    return pl.pallas_call(
        body,
        out_shape=outs,
        in_specs=specs,
        out_specs=jax.tree.map(lambda o: pl.BlockSpec(memory_space=pltpu.VMEM), outs),
        scratch_shapes=list(scratch),
        compiler_params=pltpu.CompilerParams(vmem_limit_bytes=32 * 2**20),
        cost_estimate=pl.CostEstimate(flops=flops, bytes_accessed=size, transcendentals=0),
    )


def dot(a, b, ca, cb):
    return lax.dot_general(a, b, (((ca,), (cb,)), ((), ())), preferred_element_type=F32)


def halves(x):
    high = x.astype(BF16)
    return high, (x - high.astype(F32)).astype(BF16)


def to_lanes(arrays, first):
    span = 2 * LANES * len(arrays)
    row = lax.broadcasted_iota(jnp.int32, (8, span), 0)
    group = lax.broadcasted_iota(jnp.int32, (8, span), 1) // (2 * LANES)
    pick = (row == group + first).astype(BF16)
    return dot(pick, jnp.concatenate([h for x in arrays for h in halves(x)], axis=1), 1, 1)


def to_rows(x):
    row = lax.broadcasted_iota(jnp.int32, (3, 3 * LANES), 0)
    group = lax.broadcasted_iota(jnp.int32, (3, 3 * LANES), 1) // LANES
    pick = (row == group).astype(BF16)
    high, low = halves(x)
    rows = dot(high, pick, 0, 0) + dot(low, pick, 0, 0)
    return [rows[:, i * LANES : (i + 1) * LANES] for i in range(3)]


def added(ref):
    total = ref[0]
    for i in range(1, ref.shape[0]):
        total = total + ref[i]
    return total


def inverses(ref):
    sums = to_rows(added(ref))
    widths = (HQ * HEAD_SIZE, KEY_VALUE_HEADS * HEAD_SIZE, KEY_VALUE_HEADS * HEAD_SIZE)
    return [lax.rsqrt(s / w + EPSILON) for s, w in zip(sums, widths)]


def squares_body(q_ref, k_ref, c_ref, out_ref):
    total = None
    for h in range(GROUP):
        x = q_ref[:, h * HEAD_SIZE : (h + 1) * HEAD_SIZE].astype(F32)
        total = x * x if total is None else total + x * x
    k = k_ref[...].astype(F32)
    c = c_ref[...].astype(F32)
    rows = to_lanes([total, k * k, c * c], 0)
    for peer in range(out_ref.shape[0]):
        out_ref[peer] = rows[:3]


def norms_body(
    sums_ref, q_ref, k_ref, c_ref, v_ref, cv_ref, g_ref, q_gain, k_gain, noisy_ref, out, wide, tall
):
    q_inv, k_inv, c_inv = inverses(sums_ref)
    rows = k_ref.shape[0]
    slot = up(rows, PAD)
    tall[0:rows, :LANES] = c_ref[...].astype(F32) * c_inv * k_gain[...]
    tall[0:rows, LANES:] = cv_ref[...].astype(F32)
    for h in range(GROUP):
        cols = slice(h * HEAD_SIZE, (h + 1) * HEAD_SIZE)
        gain = q_gain[:, cols] * (SCORE_SCALE * LOG2E)
        at = (1 + h) * slot
        tall[at : at + rows, :LANES] = q_ref[:, cols].astype(F32) * q_inv * gain
        tall[at : at + rows, LANES:] = g_ref[:, cols].astype(F32)
    for h in range(1 + GROUP):
        tall[h * slot + rows : (h + 1) * slot] = jnp.zeros((slot - rows, 2 * LANES), F32)
    out[...] = tall[...].astype(BF16)
    wide[rows:] = jnp.zeros((slot - rows, 2 * LANES), F32)
    wide[0:rows, 0:LANES] = k_ref[...].astype(F32) * k_inv * k_gain[...]
    wide[0:rows, LANES:] = v_ref[...].astype(F32)
    noisy_ref[...] = wide[...].astype(BF16)


def both(out, own, far):
    core = lax.axis_index("seq") % 2
    span = own.shape[0] // (1 + GROUP) * GROUP
    first = own.shape[0] - span

    @pl.when(core == 0)
    def _():
        out[0:span] = own[first:]
        out[span : 2 * span] = far[first:]

    @pl.when(core == 1)
    def _():
        out[0:span] = far[first:]
        out[span : 2 * span] = own[first:]

    out[2 * span :] = jnp.zeros((out.shape[0] - 2 * span, out.shape[1]), out.dtype)


def listed(window_ref):
    here = lax.axis_index("seq") // 2
    found = []
    for steps in (1, 2, 3):
        at = here - steps
        hit = window_ref[here, 0] == at
        for j in range(1, window_ref.shape[1]):
            hit = hit | (window_ref[here, j] == at)
        found.append(hit & (at >= 0))
    return found


def scores(key_ref, q, rows):
    whole = rows // PAD * PAD
    s = dot(key_ref[:, :LANES], q, 1, 1)
    tail = s[whole:]
    real = lax.broadcasted_iota(jnp.int32, tail.shape, 0) < rows - whole
    return s[:whole], jnp.where(real, tail, HIDDEN)


def noisy_body(own, far, keys, q_out, gt_out, e_out, sum_out, stats, rows_ref):
    both(rows_ref, own, far)
    q_out[...] = rows_ref[:, :LANES]
    gt = rows_ref[:, LANES:].astype(F32).T
    gt_out[...] = gt.astype(BF16)
    body, tail = scores(keys, q_out[...], TOKENS)
    whole = body.shape[0]
    top = jnp.maximum(
        jnp.max(body, axis=0, keepdims=True), jnp.max(tail, axis=0, keepdims=True)
    )
    body = jnp.exp2(body - top)
    tail = jnp.exp2(tail - top)
    total = jnp.sum(body, axis=0, keepdims=True) + jnp.sum(tail, axis=0, keepdims=True)
    e_out[0:whole] = body.astype(BF16)
    e_out[whole:] = tail.astype(BF16)
    sums = dot(keys[:, LANES:], e_out[...], 0, 0)
    sum_out[...] = sums
    stats[...] = jnp.zeros_like(stats)
    stats[0:1] = top
    stats[1:2] = total
    stats[2:3] = jnp.sum(gt * sums, axis=0, keepdims=True)


def pair_body(own, far, out):
    rows = out.shape[1]
    slot = up(rows, PAD)
    for j, ref in enumerate((own, far)):
        out[j] = ref[0:slot].astype(F32)[:rows].astype(BF16)


def clean_body(
    window_ref, near, far, q_ref, gt_ref, noisy_stats, keys, e_out, dp_out, stats, s_ref
):
    use1, use2, use3 = listed(window_ref)
    first = lax.axis_index("seq") % 2 == 0
    from_far = jnp.logical_not(first) & use2

    def take(ref):
        rows = ref.shape[1]
        for j in range(2):
            s_ref[j, 0:rows, 0 : 2 * LANES] = ref[j].astype(F32)
            s_ref[j, rows:, 0 : 2 * LANES] = jnp.zeros_like(s_ref[j, rows:, 0 : 2 * LANES])
            keys[j] = s_ref[j, :, 0 : 2 * LANES].astype(BF16)

    @pl.when(from_far)
    def _():
        take(far)

    @pl.when(jnp.logical_not(from_far))
    def _():
        take(near)

    hide = jnp.where(jnp.where(first, use1, use2 | use3), 0.0, HIDDEN)
    q = q_ref[...]
    top = None
    for j in range(2):
        body, tail = scores(keys.at[j], q, TOKENS)
        whole = body.shape[0]
        body = body + hide
        tail = tail + hide
        s_ref[j, 0:whole] = body
        s_ref[j, whole:] = tail
        here = jnp.maximum(
            jnp.max(body, axis=0, keepdims=True), jnp.max(tail, axis=0, keepdims=True)
        )
        top = here if top is None else jnp.maximum(top, here)
    total = None
    delta = None
    for j in range(2):
        e = jnp.exp2(s_ref[j] - top)
        e_out[j] = e.astype(BF16)
        dp = dot(keys[j, :, LANES:], gt_ref[...], 1, 0)
        dp_out[j] = dp
        part = jnp.sum(e, axis=0, keepdims=True)
        share = jnp.sum(e * dp, axis=0, keepdims=True)
        total = part if total is None else total + part
        delta = share if delta is None else delta + share
    stats[...] = noisy_stats[...]
    stats[3:4] = top
    stats[4:5] = total
    stats[5:6] = delta


def clean_grad_body(
    window_ref, own, far, q_ref, gt_ref, dp_ref, e_ref, near_out, far_out, ds_out, merged
):
    use1, use2, use3 = listed(window_ref)
    first = lax.axis_index("seq") % 2 == 0
    groups = [(ref[i : i + 1], ref[i + 1 : i + 2], ref[i + 2 : i + 3])
              for ref in (own, far) for i in (0, 3)]
    top = groups[0][0]
    for group in groups[1:]:
        top = jnp.maximum(top, group[0])
    weights = [jnp.exp2(group[0] - top) for group in groups]
    inv = 1.0 / sum(w * group[1] for w, group in zip(weights, groups))
    delta = sum(w * group[2] for w, group in zip(weights, groups)) * inv
    noisy, clean = weights[0] * inv, weights[1] * inv
    merged[...] = jnp.zeros_like(merged)
    merged[0:1] = noisy
    merged[1:2] = clean
    merged[2:3] = delta * noisy
    gt = (gt_ref[...].astype(F32) * clean).astype(BF16)
    delta = delta * clean
    q = q_ref[...]
    rows = near_out.shape[1]
    keep_near = jnp.where(jnp.where(first, use1, use3), 1.0, 0.0)
    keep_far = jnp.where(use2, 1.0, 0.0)
    for j in range(2):
        e = e_ref[j]
        ds = (e.astype(F32) * (dp_ref[j] * clean - delta)).astype(BF16)
        ds_out[j] = ds
        dk = dot(ds, q, 1, 0) * (1.0 / LOG2E)
        dv = dot(e, gt, 1, 1)
        for out, keep in ((near_out, keep_near), (far_out, keep_far)):
            out[j, :, :LANES] = (dk[:rows] * keep).astype(BF16)
            out[j, :, LANES:] = (dv[:rows] * keep).astype(BF16)


def noisy_grad_body(
    merged, q_ref, gt_ref, keys, clean_keys, e_ref, clean_e, ds_ref, noisy_sum,
    grads, own, far, wide,
):
    core = lax.axis_index("seq") % 2
    span = own.shape[0] // 2
    mine = pl.ds(pl.multiple_of(core * span, 8), span)
    theirs = pl.ds(pl.multiple_of((1 - core) * span, 8), span)
    noisy = merged[0:1]
    gt = (gt_ref[...].astype(F32) * noisy).astype(BF16)
    e = e_ref[...]
    dp = dot(keys[:, LANES:], gt, 1, 0)
    ds = (e.astype(F32) * (dp - merged[2:3])).astype(BF16)
    dk = dot(ds, q_ref[...], 1, 0) * (1.0 / LOG2E)
    dv = dot(e, gt, 1, 1)
    rows = grads.shape[0]
    grads[:, :LANES] = dk[:rows]
    grads[:, LANES:] = dv[:rows]
    dq = dot(keys[:, :LANES], ds, 0, 0)
    for j in range(2):
        dq = dq + dot(clean_keys[j, :, :LANES], ds_ref[j], 0, 0)
    clean_sum = dot(clean_keys[0, :, LANES:], clean_e[0], 0, 0)
    clean_sum = clean_sum + dot(clean_keys[1, :, LANES:], clean_e[1], 0, 0)
    wide[0] = (noisy_sum[...] * noisy + clean_sum * merged[1:2]).T
    wide[1] = (dq * SCORE_SCALE).T
    for i in range(2):
        own[i * span : (i + 1) * span] = wide[i, mine]
        far[i * span : (i + 1) * span] = wide[i, theirs].astype(BF16)


def join_body(near, far, own_out, far_out):
    own_out[...] = near[0].astype(F32) + far[0].astype(F32)
    far_out[...] = (near[1].astype(F32) + far[1].astype(F32)).astype(BF16)


def settle_body(
    sums_ref, own, far, grads, q_ref, k_ref, c_ref, q_gain, k_gain,
    attn_out, grad_v, sums, q_push, q_pull, k_push, k_pull, c_scale, c_pull,
):
    q_inv, k_inv, c_inv = inverses(sums_ref)
    grad_v[...] = grads[:, LANES:].astype(BF16)
    span = own.shape[0] // 2
    slot = span // GROUP
    rows = attn_out.shape[0]
    total = own[...] + far[...].astype(F32)
    cube = q_inv * q_inv * q_inv * (1.0 / (HQ * HEAD_SIZE))
    inner = None
    for h in range(GROUP):
        cols = slice(h * HEAD_SIZE, (h + 1) * HEAD_SIZE)
        attn_out[:, cols] = total[h * slot : h * slot + rows].astype(BF16)
        at = span + h * slot
        scaled = total[at : at + rows] * q_gain[:, cols]
        x = q_ref[:, cols].astype(F32)
        q_push[:, cols] = scaled * q_inv
        q_pull[:, cols] = x * cube
        inner = scaled * x if inner is None else inner + scaled * x
    width = 1.0 / (KEY_VALUE_HEADS * HEAD_SIZE)
    x = k_ref[...].astype(F32)
    scaled = grads[:, :LANES] * k_gain[...]
    k_push[...] = scaled * k_inv
    k_pull[...] = x * (k_inv * k_inv * k_inv * width)
    c_scale[...] = c_inv
    c_pull[...] = c_ref[...].astype(F32) * (c_inv * c_inv * c_inv * width)
    sums[...] = to_lanes([inner, scaled * x], 0)


def inner_body(own_clean, far_clean, c_ref, k_gain, c_scale, sums, c_push, grad_cv, out_ref):
    clean = own_clean[...] + far_clean[...].astype(F32)
    grad_cv[...] = clean[:, LANES:].astype(BF16)
    scaled = clean[:, :LANES] * k_gain[...]
    c_push[...] = scaled * c_scale[...]
    part = sums[...] + to_lanes([scaled * c_ref[...].astype(F32)], 2)
    for peer in range(out_ref.shape[0]):
        out_ref[peer] = part[:3]


def finish_body(
    inner_ref, q_push, q_pull, k_push, k_pull, c_push, c_pull, grad_q, grad_k, grad_ck
):
    q_sum, k_sum, c_sum = to_rows(added(inner_ref))
    for h in range(GROUP):
        cols = slice(h * HEAD_SIZE, (h + 1) * HEAD_SIZE)
        grad_q[:, cols] = (q_push[:, cols] - q_pull[:, cols] * q_sum).astype(BF16)
    grad_k[...] = (k_push[...] - k_pull[...] * k_sum).astype(BF16)
    grad_ck[...] = (c_push[...] - c_pull[...] * c_sum).astype(BF16)


def head_exchange(value):
    return lax.all_to_all(value, "head", 0, 0)


def stretch_shift(value, steps, far):
    count = lax.axis_size("seq")
    pairs = []
    for i in range(count):
        if far and i % 2 == 0:
            continue
        length = 2 if far else (1, 3)[i % 2]
        target = i + 2 * length * steps
        if 0 <= target < count:
            pairs.append((i, target))
    return lax.ppermute(value, "seq", pairs)


def core_swap(value):
    count = lax.axis_size("seq")
    return lax.ppermute(value, "seq", [(i, i ^ 1) for i in range(count)])


def on_device(
    noisy_q, noisy_k, noisy_value, clean_k, clean_value, q_gain, key_norm_gain, out_grad, window
):
    rows = noisy_q.shape[0]
    slot = up(rows, PAD)
    span = GROUP * slot
    queries = up(2 * span, LANES)
    peers = lax.axis_size("head")
    q_gain = q_gain[None, :]
    k_gain = key_norm_gain[None, :]
    product = 2 * slot * queries * LANES
    stats = shape((8, queries), F32)
    turned = shape((LANES, queries), F32)

    fetched = (noisy_q, noisy_k, clean_k)
    sums = pl.pallas_call(
        squares_body,
        grid=(1,),
        out_shape=shape((peers, 3, rows), F32),
        in_specs=[pl.BlockSpec(a.shape, lambda i: (0, 0)) for a in fetched],
        out_specs=pl.BlockSpec((peers, 3, rows), lambda i: (0, 0, 0)),
        compiler_params=pltpu.CompilerParams(vmem_limit_bytes=60 * 2**20),
        cost_estimate=pl.CostEstimate(flops=10**10, bytes_accessed=10**6, transcendentals=0),
    )(*fetched)
    sums = head_exchange(sums)
    pack = shape((slot, 2 * LANES), BF16)
    packed = ((1 + GROUP) * slot, 2 * LANES)
    noisy_kv, own = kernel_call(
        norms_body,
        (pack, shape(packed, BF16)),
        10**6,
        [pltpu.VMEM((slot, 2 * LANES), F32), pltpu.VMEM(packed, F32)],
        nargs=9,
    )(sums, noisy_q, noisy_k, clean_k, noisy_value, clean_value, out_grad, q_gain, k_gain)
    far = core_swap(own)
    pair_kv = shape((2, slot, 2 * LANES), BF16)
    flown = shape((2, rows, 2 * LANES), BF16)
    clean_kv = kernel_call(pair_body, flown, 10**6, nargs=2)(own, far)
    near_kv = stretch_shift(clean_kv, 1, False)
    far_kv = stretch_shift(clean_kv, 1, True)
    q_all, g_turned, noisy_e, noisy_sum, noisy_stats = kernel_call(
        noisy_body,
        (
            shape((queries, LANES), BF16),
            shape((LANES, queries), BF16),
            shape((slot, queries), BF16),
            turned,
            stats,
        ),
        4 * product,
        [pltpu.VMEM((queries, 2 * LANES), BF16)],
        nargs=3,
    )(own, far, noisy_kv)
    pair = shape((2, slot, queries), BF16)
    keys, clean_e, products, own_stats = kernel_call(
        clean_body,
        (pair_kv, pair, shape((2, slot, queries), F32), stats),
        8 * product,
        [pltpu.VMEM((2, slot, queries), F32)],
        smem=(0,),
        nargs=6,
    )(window, near_kv, far_kv, q_all, g_turned, noisy_stats)
    far_stats = core_swap(own_stats)
    pair_grad = shape((2, rows, 2 * LANES), BF16)
    near_back, far_back, clean_ds, merged = kernel_call(
        clean_grad_body,
        (pair_grad, pair_grad, pair, stats),
        8 * product,
        smem=(0,),
        nargs=7,
    )(window, own_stats, far_stats, q_all, g_turned, products, clean_e)
    near_back = stretch_shift(near_back, -1, False)
    far_back = stretch_shift(far_back, -1, True)
    noisy_grads, own, far = kernel_call(
        noisy_grad_body,
        (
            shape((rows, 2 * LANES), F32),
            shape((2 * span, LANES), F32),
            shape((2 * span, LANES), BF16),
        ),
        8 * product,
        [pltpu.VMEM((2, queries, LANES), F32)],
        nargs=9,
    )(merged, q_all, g_turned, noisy_kv, keys, noisy_e, clean_e, clean_ds, noisy_sum)
    far = core_swap(far)
    key_grad = shape((rows, LANES), BF16)
    query_grad = shape((rows, GROUP * LANES), BF16)
    own_clean, far_clean = kernel_call(
        join_body,
        (shape((rows, 2 * LANES), F32), shape((rows, 2 * LANES), BF16)),
        10**10,
        nargs=2,
    )(near_back, far_back)
    far_clean = core_swap(far_clean)
    query_wide = shape((rows, GROUP * LANES), F32)
    key_wide = shape((rows, LANES), F32)
    attn_out, grad_v, inner, q_push, q_pull, k_push, k_pull, c_scale, c_pull = kernel_call(
        settle_body,
        (query_grad, key_grad, shape((8, rows), F32), query_wide, query_wide)
        + (key_wide,) * 4,
        10**6,
        nargs=9,
    )(sums, own, far, noisy_grads, noisy_q, noisy_k, clean_k, q_gain, k_gain)
    c_push, grad_cv, inner = kernel_call(
        inner_body,
        (key_wide, key_grad, shape((peers, 3, rows), F32)),
        10**6,
        nargs=6,
    )(own_clean, far_clean, clean_k, k_gain, c_scale, inner)
    inner = head_exchange(inner)
    grad_q, grad_k, grad_ck = kernel_call(
        finish_body, (query_grad, key_grad, key_grad), 10**6, nargs=7
    )(inner, q_push, q_pull, k_push, k_pull, c_push, c_pull)
    return (attn_out, grad_q, grad_k, grad_v, grad_ck, grad_cv)


def solution(mesh):
    tokens = P("seq", "head")
    return jax.shard_map(
        on_device,
        mesh=mesh,
        in_specs=(tokens,) * 5 + (P("head"), P("head"), tokens, P()),
        out_specs=(tokens,) * 6,
        check_vma=False,
    )
```

```python
import math

import jax
import jax.numpy as jnp
from jax import lax
from jax.experimental import pallas as pl
from jax.experimental.pallas import tpu as pltpu
from jax.sharding import PartitionSpec as P

HEAD_SIZE = 128
KEY_VALUE_HEADS = 8
GROUP = 3
STRETCH = 520
HQ = 24
TOKENS = STRETCH // 2
EPSILON = 1e-06
HIDDEN = -1e30

PAD = 16
LANES = 128
F32 = jnp.float32
BF16 = jnp.bfloat16
SCORE_SCALE = HEAD_SIZE ** (-0.5)
LOG2E = math.log2(math.e)


def up(count, unit):
    return -(-count // unit) * unit


def shape(dims, kind):
    return jax.ShapeDtypeStruct(dims, kind)


def kernel_call(body, outs, flops, scratch=(), smem=(), nargs=0):
    specs = [pl.BlockSpec(memory_space=pltpu.SMEM if i in smem else pltpu.VMEM) for i in range(nargs)]
    size = sum(math.prod(o.shape) * o.dtype.itemsize for o in jax.tree.leaves(outs))
    return pl.pallas_call(
        body,
        out_shape=outs,
        in_specs=specs,
        out_specs=jax.tree.map(lambda o: pl.BlockSpec(memory_space=pltpu.VMEM), outs),
        scratch_shapes=list(scratch),
        compiler_params=pltpu.CompilerParams(vmem_limit_bytes=32 * 2**20),
        cost_estimate=pl.CostEstimate(flops=flops, bytes_accessed=size, transcendentals=0),
    )


def dot(a, b, ca, cb):
    return lax.dot_general(a, b, (((ca,), (cb,)), ((), ())), preferred_element_type=F32)


def halves(x):
    high = x.astype(BF16)
    return high, (x - high.astype(F32)).astype(BF16)


def to_lanes(arrays, first):
    span = 2 * LANES * len(arrays)
    row = lax.broadcasted_iota(jnp.int32, (8, span), 0)
    group = lax.broadcasted_iota(jnp.int32, (8, span), 1) // (2 * LANES)
    pick = (row == group + first).astype(BF16)
    return dot(pick, jnp.concatenate([h for x in arrays for h in halves(x)], axis=1), 1, 1)


def to_rows(x):
    row = lax.broadcasted_iota(jnp.int32, (3, 3 * LANES), 0)
    group = lax.broadcasted_iota(jnp.int32, (3, 3 * LANES), 1) // LANES
    pick = (row == group).astype(BF16)
    high, low = halves(x)
    rows = dot(high, pick, 0, 0) + dot(low, pick, 0, 0)
    return [rows[:, i * LANES : (i + 1) * LANES] for i in range(3)]


def added(ref):
    total = ref[0]
    for i in range(1, ref.shape[0]):
        total = total + ref[i]
    return total


def inverses(ref):
    sums = to_rows(added(ref))
    widths = (HQ * HEAD_SIZE, KEY_VALUE_HEADS * HEAD_SIZE, KEY_VALUE_HEADS * HEAD_SIZE)
    return [lax.rsqrt(s / w + EPSILON) for s, w in zip(sums, widths)]


def squares_body(q_ref, k_ref, c_ref, out_ref):
    total = None
    for h in range(GROUP):
        x = q_ref[:, h * HEAD_SIZE : (h + 1) * HEAD_SIZE].astype(F32)
        total = x * x if total is None else total + x * x
    k = k_ref[...].astype(F32)
    c = c_ref[...].astype(F32)
    rows = to_lanes([total, k * k, c * c], 0)
    for peer in range(out_ref.shape[0]):
        out_ref[peer] = rows[:3]


def norms_body(
    sums_ref, q_ref, k_ref, c_ref, v_ref, cv_ref, g_ref, q_gain, k_gain, noisy_ref, out, wide, tall
):
    q_inv, k_inv, c_inv = inverses(sums_ref)
    rows = k_ref.shape[0]
    slot = up(rows, PAD)
    tall[0:rows, :LANES] = c_ref[...].astype(F32) * c_inv * k_gain[...]
    tall[0:rows, LANES:] = cv_ref[...].astype(F32)
    for h in range(GROUP):
        cols = slice(h * HEAD_SIZE, (h + 1) * HEAD_SIZE)
        gain = q_gain[:, cols] * (SCORE_SCALE * LOG2E)
        at = (1 + h) * slot
        tall[at : at + rows, :LANES] = q_ref[:, cols].astype(F32) * q_inv * gain
        tall[at : at + rows, LANES:] = g_ref[:, cols].astype(F32)
    for h in range(1 + GROUP):
        tall[h * slot + rows : (h + 1) * slot] = jnp.zeros((slot - rows, 2 * LANES), F32)
    out[...] = tall[...].astype(BF16)
    wide[rows:] = jnp.zeros((slot - rows, 2 * LANES), F32)
    wide[0:rows, 0:LANES] = k_ref[...].astype(F32) * k_inv * k_gain[...]
    wide[0:rows, LANES:] = v_ref[...].astype(F32)
    noisy_ref[...] = wide[...].astype(BF16)


def both(out, own, far):
    core = lax.axis_index("seq") % 2
    span = own.shape[0] // (1 + GROUP) * GROUP
    first = own.shape[0] - span

    @pl.when(core == 0)
    def _():
        out[0:span] = own[first:]
        out[span : 2 * span] = far[first:]

    @pl.when(core == 1)
    def _():
        out[0:span] = far[first:]
        out[span : 2 * span] = own[first:]

    out[2 * span :] = jnp.zeros((out.shape[0] - 2 * span, out.shape[1]), out.dtype)


def listed(window_ref):
    here = lax.axis_index("seq") // 2
    found = []
    for steps in (1, 2, 3):
        at = here - steps
        hit = window_ref[here, 0] == at
        for j in range(1, window_ref.shape[1]):
            hit = hit | (window_ref[here, j] == at)
        found.append(hit & (at >= 0))
    return found


def scores(key_ref, q, rows):
    whole = rows // PAD * PAD
    s = dot(key_ref[:, :LANES], q, 1, 1)
    tail = s[whole:]
    real = lax.broadcasted_iota(jnp.int32, tail.shape, 0) < rows - whole
    return s[:whole], jnp.where(real, tail, HIDDEN)


def noisy_body(own, far, keys, q_out, gt_out, e_out, sum_out, stats, rows_ref):
    both(rows_ref, own, far)
    q_out[...] = rows_ref[:, :LANES]
    gt = rows_ref[:, LANES:].astype(F32).T
    gt_out[...] = gt.astype(BF16)
    body, tail = scores(keys, q_out[...], TOKENS)
    whole = body.shape[0]
    top = jnp.maximum(
        jnp.max(body, axis=0, keepdims=True), jnp.max(tail, axis=0, keepdims=True)
    )
    body = jnp.exp2(body - top)
    tail = jnp.exp2(tail - top)
    total = jnp.sum(body, axis=0, keepdims=True) + jnp.sum(tail, axis=0, keepdims=True)
    e_out[0:whole] = body.astype(BF16)
    e_out[whole:] = tail.astype(BF16)
    sums = dot(keys[:, LANES:], e_out[...], 0, 0)
    sum_out[...] = sums
    stats[...] = jnp.zeros_like(stats)
    stats[0:1] = top
    stats[1:2] = total
    stats[2:3] = jnp.sum(gt * sums, axis=0, keepdims=True)


def pair_body(own, far, out):
    rows = out.shape[1]
    slot = up(rows, PAD)
    for j, ref in enumerate((own, far)):
        out[j] = ref[0:slot].astype(F32)[:rows].astype(BF16)


def clean_body(
    window_ref, far, near, q_ref, gt_ref, noisy_stats, keys, e_out, dp_out, stats, s_ref
):
    use1, use2, use3 = listed(window_ref)
    first = lax.axis_index("seq") % 2 == 0
    from_far = jnp.logical_not(first) & use2

    def take(ref):
        rows = ref.shape[1]
        for j in range(2):
            s_ref[j, 0:rows, 0 : 2 * LANES] = ref[j].astype(F32)
            s_ref[j, rows:, 0 : 2 * LANES] = jnp.zeros_like(s_ref[j, rows:, 0 : 2 * LANES])
            keys[j] = s_ref[j, :, 0 : 2 * LANES].astype(BF16)

    @pl.when(from_far)
    def _():
        take(far)

    @pl.when(jnp.logical_not(from_far))
    def _():
        take(near)

    hide = jnp.where(jnp.where(first, use1, use2 | use3), 0.0, HIDDEN)
    q = q_ref[...]
    top = None
    for j in range(2):
        body, tail = scores(keys.at[j], q, TOKENS)
        whole = body.shape[0]
        body = body + hide
        tail = tail + hide
        s_ref[j, 0:whole] = body
        s_ref[j, whole:] = tail
        here = jnp.maximum(
            jnp.max(body, axis=0, keepdims=True), jnp.max(tail, axis=0, keepdims=True)
        )
        top = here if top is None else jnp.maximum(top, here)
    total = None
    delta = None
    for j in range(2):
        e = jnp.exp2(s_ref[j] - top)
        e_out[j] = e.astype(BF16)
        dp = dot(keys[j, :, LANES:], gt_ref[...], 1, 0)
        dp_out[j] = dp
        part = jnp.sum(e, axis=0, keepdims=True)
        share = jnp.sum(e * dp, axis=0, keepdims=True)
        total = part if total is None else total + part
        delta = share if delta is None else delta + share
    stats[...] = noisy_stats[...]
    stats[3:4] = top
    stats[4:5] = total
    stats[5:6] = delta


def clean_grad_body(
    window_ref, own, far, q_ref, gt_ref, dp_ref, e_ref, near_out, far_out, ds_out, merged
):
    use1, use2, use3 = listed(window_ref)
    first = lax.axis_index("seq") % 2 == 0
    groups = [(ref[i : i + 1], ref[i + 1 : i + 2], ref[i + 2 : i + 3])
              for ref in (own, far) for i in (0, 3)]
    top = groups[0][0]
    for group in groups[1:]:
        top = jnp.maximum(top, group[0])
    weights = [jnp.exp2(group[0] - top) for group in groups]
    inv = 1.0 / sum(w * group[1] for w, group in zip(weights, groups))
    delta = sum(w * group[2] for w, group in zip(weights, groups)) * inv
    noisy, clean = weights[0] * inv, weights[1] * inv
    merged[...] = jnp.zeros_like(merged)
    merged[0:1] = noisy
    merged[1:2] = clean
    merged[2:3] = delta * noisy
    gt = (gt_ref[...].astype(F32) * clean).astype(BF16)
    delta = delta * clean
    q = q_ref[...]
    rows = near_out.shape[1]
    keep_near = jnp.where(jnp.where(first, use1, use3), 1.0, 0.0)
    keep_far = jnp.where(use2, 1.0, 0.0)
    for j in range(2):
        e = e_ref[j]
        ds = (e.astype(F32) * (dp_ref[j] * clean - delta)).astype(BF16)
        ds_out[j] = ds
        dk = dot(ds, q, 1, 0) * (1.0 / LOG2E)
        dv = dot(e, gt, 1, 1)
        for out, keep in ((near_out, keep_near), (far_out, keep_far)):
            out[j, :, :LANES] = (dk[:rows] * keep).astype(BF16)
            out[j, :, LANES:] = (dv[:rows] * keep).astype(BF16)


def noisy_grad_body(
    merged, q_ref, gt_ref, keys, clean_keys, e_ref, clean_e, ds_ref, noisy_sum,
    grads, own, far, wide,
):
    core = lax.axis_index("seq") % 2
    span = own.shape[0] // 2
    mine = pl.ds(pl.multiple_of(core * span, 8), span)
    theirs = pl.ds(pl.multiple_of((1 - core) * span, 8), span)
    noisy = merged[0:1]
    gt = (gt_ref[...].astype(F32) * noisy).astype(BF16)
    e = e_ref[...]
    dp = dot(keys[:, LANES:], gt, 1, 0)
    ds = (e.astype(F32) * (dp - merged[2:3])).astype(BF16)
    dk = dot(ds, q_ref[...], 1, 0) * (1.0 / LOG2E)
    dv = dot(e, gt, 1, 1)
    rows = grads.shape[0]
    grads[:, :LANES] = dk[:rows]
    grads[:, LANES:] = dv[:rows]
    dq = dot(keys[:, :LANES], ds, 0, 0)
    for j in range(2):
        dq = dq + dot(clean_keys[j, :, :LANES], ds_ref[j], 0, 0)
    clean_sum = dot(clean_keys[0, :, LANES:], clean_e[0], 0, 0)
    clean_sum = clean_sum + dot(clean_keys[1, :, LANES:], clean_e[1], 0, 0)
    wide[0] = (noisy_sum[...] * noisy + clean_sum * merged[1:2]).T
    wide[1] = (dq * SCORE_SCALE).T
    for i in range(2):
        own[i * span : (i + 1) * span] = wide[i, mine]
        far[i * span : (i + 1) * span] = wide[i, theirs].astype(BF16)


def join_body(near, far, own_out, far_out):
    own_out[...] = near[0].astype(F32) + far[0].astype(F32)
    far_out[...] = (near[1].astype(F32) + far[1].astype(F32)).astype(BF16)


def settle_body(
    sums_ref, own, far, grads, q_ref, k_ref, c_ref, q_gain, k_gain,
    attn_out, grad_v, sums, q_push, q_pull, k_push, k_pull, c_scale, c_pull,
):
    q_inv, k_inv, c_inv = inverses(sums_ref)
    grad_v[...] = grads[:, LANES:].astype(BF16)
    span = own.shape[0] // 2
    slot = span // GROUP
    rows = attn_out.shape[0]
    total = own[...] + far[...].astype(F32)
    cube = q_inv * q_inv * q_inv * (1.0 / (HQ * HEAD_SIZE))
    inner = None
    for h in range(GROUP):
        cols = slice(h * HEAD_SIZE, (h + 1) * HEAD_SIZE)
        attn_out[:, cols] = total[h * slot : h * slot + rows].astype(BF16)
        at = span + h * slot
        scaled = total[at : at + rows] * q_gain[:, cols]
        x = q_ref[:, cols].astype(F32)
        q_push[:, cols] = scaled * q_inv
        q_pull[:, cols] = x * cube
        inner = scaled * x if inner is None else inner + scaled * x
    width = 1.0 / (KEY_VALUE_HEADS * HEAD_SIZE)
    x = k_ref[...].astype(F32)
    scaled = grads[:, :LANES] * k_gain[...]
    k_push[...] = scaled * k_inv
    k_pull[...] = x * (k_inv * k_inv * k_inv * width)
    c_scale[...] = c_inv
    c_pull[...] = c_ref[...].astype(F32) * (c_inv * c_inv * c_inv * width)
    sums[...] = to_lanes([inner, scaled * x], 0)


def inner_body(own_clean, far_clean, c_ref, k_gain, c_scale, sums, c_push, grad_cv, out_ref):
    clean = own_clean[...] + far_clean[...].astype(F32)
    grad_cv[...] = clean[:, LANES:].astype(BF16)
    scaled = clean[:, :LANES] * k_gain[...]
    c_push[...] = scaled * c_scale[...]
    part = sums[...] + to_lanes([scaled * c_ref[...].astype(F32)], 2)
    for peer in range(out_ref.shape[0]):
        out_ref[peer] = part[:3]


def finish_body(
    inner_ref, q_push, q_pull, k_push, k_pull, c_push, c_pull, grad_q, grad_k, grad_ck
):
    q_sum, k_sum, c_sum = to_rows(added(inner_ref))
    for h in range(GROUP):
        cols = slice(h * HEAD_SIZE, (h + 1) * HEAD_SIZE)
        grad_q[:, cols] = (q_push[:, cols] - q_pull[:, cols] * q_sum).astype(BF16)
    grad_k[...] = (k_push[...] - k_pull[...] * k_sum).astype(BF16)
    grad_ck[...] = (c_push[...] - c_pull[...] * c_sum).astype(BF16)


def head_exchange(value):
    return lax.all_to_all(value, "head", 0, 0)


def stretch_shift(value, steps, far):
    count = lax.axis_size("seq")
    pairs = []
    for i in range(count):
        if far and i % 2 == 0:
            continue
        length = 2 if far else (1, 3)[i % 2]
        target = i + 2 * length * steps
        if 0 <= target < count:
            pairs.append((i, target))
    return lax.ppermute(value, "seq", pairs)


def core_swap(value):
    count = lax.axis_size("seq")
    return lax.ppermute(value, "seq", [(i, i ^ 1) for i in range(count)])


def on_device(
    noisy_q, noisy_k, noisy_value, clean_k, clean_value, q_gain, key_norm_gain, out_grad, window
):
    rows = noisy_q.shape[0]
    slot = up(rows, PAD)
    span = GROUP * slot
    queries = up(2 * span, LANES)
    peers = lax.axis_size("head")
    q_gain = q_gain[None, :]
    k_gain = key_norm_gain[None, :]
    product = 2 * slot * queries * LANES
    stats = shape((8, queries), F32)
    turned = shape((LANES, queries), F32)

    fetched = (noisy_q, noisy_k, clean_k)
    sums = pl.pallas_call(
        squares_body,
        grid=(1,),
        out_shape=shape((peers, 3, rows), F32),
        in_specs=[pl.BlockSpec(a.shape, lambda i: (0, 0)) for a in fetched],
        out_specs=pl.BlockSpec((peers, 3, rows), lambda i: (0, 0, 0)),
        compiler_params=pltpu.CompilerParams(vmem_limit_bytes=60 * 2**20),
        cost_estimate=pl.CostEstimate(flops=10**10, bytes_accessed=10**6, transcendentals=0),
    )(*fetched)
    sums = head_exchange(sums)
    pack = shape((slot, 2 * LANES), BF16)
    packed = ((1 + GROUP) * slot, 2 * LANES)
    noisy_kv, own = kernel_call(
        norms_body,
        (pack, shape(packed, BF16)),
        10**6,
        [pltpu.VMEM((slot, 2 * LANES), F32), pltpu.VMEM(packed, F32)],
        nargs=9,
    )(sums, noisy_q, noisy_k, clean_k, noisy_value, clean_value, out_grad, q_gain, k_gain)
    far = core_swap(own)
    pair_kv = shape((2, slot, 2 * LANES), BF16)
    flown = shape((2, rows, 2 * LANES), BF16)
    clean_kv = kernel_call(pair_body, flown, 10**6, nargs=2)(own, far)
    far_kv = stretch_shift(clean_kv, 1, True)
    near_kv = stretch_shift(clean_kv, 1, False)
    q_all, g_turned, noisy_e, noisy_sum, noisy_stats = kernel_call(
        noisy_body,
        (
            shape((queries, LANES), BF16),
            shape((LANES, queries), BF16),
            shape((slot, queries), BF16),
            turned,
            stats,
        ),
        4 * product,
        [pltpu.VMEM((queries, 2 * LANES), BF16)],
        nargs=3,
    )(own, far, noisy_kv)
    pair = shape((2, slot, queries), BF16)
    keys, clean_e, products, own_stats = kernel_call(
        clean_body,
        (pair_kv, pair, shape((2, slot, queries), F32), stats),
        8 * product,
        [pltpu.VMEM((2, slot, queries), F32)],
        smem=(0,),
        nargs=6,
    )(window, far_kv, near_kv, q_all, g_turned, noisy_stats)
    far_stats = core_swap(own_stats)
    pair_grad = shape((2, rows, 2 * LANES), BF16)
    near_back, far_back, clean_ds, merged = kernel_call(
        clean_grad_body,
        (pair_grad, pair_grad, pair, stats),
        8 * product,
        smem=(0,),
        nargs=7,
    )(window, own_stats, far_stats, q_all, g_turned, products, clean_e)
    near_back = stretch_shift(near_back, -1, False)
    far_back = stretch_shift(far_back, -1, True)
    noisy_grads, own, far = kernel_call(
        noisy_grad_body,
        (
            shape((rows, 2 * LANES), F32),
            shape((2 * span, LANES), F32),
            shape((2 * span, LANES), BF16),
        ),
        8 * product,
        [pltpu.VMEM((2, queries, LANES), F32)],
        nargs=9,
    )(merged, q_all, g_turned, noisy_kv, keys, noisy_e, clean_e, clean_ds, noisy_sum)
    far = core_swap(far)
    key_grad = shape((rows, LANES), BF16)
    query_grad = shape((rows, GROUP * LANES), BF16)
    own_clean, far_clean = kernel_call(
        join_body,
        (shape((rows, 2 * LANES), F32), shape((rows, 2 * LANES), BF16)),
        10**10,
        nargs=2,
    )(near_back, far_back)
    far_clean = core_swap(far_clean)
    query_wide = shape((rows, GROUP * LANES), F32)
    key_wide = shape((rows, LANES), F32)
    attn_out, grad_v, inner, q_push, q_pull, k_push, k_pull, c_scale, c_pull = kernel_call(
        settle_body,
        (query_grad, key_grad, shape((8, rows), F32), query_wide, query_wide)
        + (key_wide,) * 4,
        10**6,
        nargs=9,
    )(sums, own, far, noisy_grads, noisy_q, noisy_k, clean_k, q_gain, k_gain)
    c_push, grad_cv, inner = kernel_call(
        inner_body,
        (key_wide, key_grad, shape((peers, 3, rows), F32)),
        10**6,
        nargs=6,
    )(own_clean, far_clean, clean_k, k_gain, c_scale, inner)
    inner = head_exchange(inner)
    grad_q, grad_k, grad_ck = kernel_call(
        finish_body, (query_grad, key_grad, key_grad), 10**6, nargs=7
    )(inner, q_push, q_pull, k_push, k_pull, c_push, c_pull)
    return (attn_out, grad_q, grad_k, grad_v, grad_ck, grad_cv)


def solution(mesh):
    tokens = P("seq", "head")
    return jax.shard_map(
        on_device,
        mesh=mesh,
        in_specs=(tokens,) * 5 + (P("head"), P("head"), tokens, P()),
        out_specs=(tokens,) * 6,
        check_vma=False,
    )
```
